32 devices in a mesh: curve: 32 (over z, y, x, core).
Axes of the slice: x: 2, y: 2, z: 4, core: 2. Of those that a mesh axis runs over, the one named last changes fastest.
Arguments:
- fields: float32 [128, 6, 128, 128], P('curve'), as said below
- wet_mask: int32 [128, 128, 128], P('curve'), may hold values 0 or 1
- neighbors: int32 [128, 4], replicated, may hold values from -1 to 127, as said below
- migration: int32 [32, 1], replicated, may hold values from 0 to 3, as said below
Outputs:
- final_fields: float32 [128, 6, 128, 128], P('curve')
The draws below stay inside these ranges and needn't reach their ends.
Inputs may be any that keep to these rules, and one draw needn't show every extreme that they name: `fields`: field 0 (depth) is 0.3 or more before masking, field 5 lies between 0.01 and 0.1. The patches form a rectangular grid; row p names its west, east, south and north neighbors, -1 at the grid's boundary, and the relation is symmetric. Row d names 1 different slots of owner d; the patch in slot migration[d, k] moves to owner d + 1 (owner 0 after the last) and takes slot migration[d + 1, k] there.
All inputs are finite; a program needn't handle non-finite values. No bound on the sum of `wet_mask` on one device may be relied on, other than what follows from the above.
Results may differ from the reference program's by a relative error of at most 0.00002.
Values sent between devices are 32-bit elements; how exact they have to be, the bound alone decides.
A program may use at most 128 MiB of HBM per device.

```python
import math
import jax
import jax.numpy as jnp
from jax import lax

PS = 128
P_DEV = 4
MIG = 1
OWNERS = 32
PATCHES = 128


def draw_fields(key, part):
    subkeys = jax.random.split(key, 6)
    extent = (PATCHES, PS, PS)
    water = 0.5 + 2.0 * jax.random.uniform(subkeys[0], extent)
    flow_x = water * 0.3 * jnp.clip(jax.random.normal(subkeys[1], extent), -3.0, 3.0)
    flow_y = water * 0.3 * jnp.clip(jax.random.normal(subkeys[2], extent), -3.0, 3.0)
    bed_level = 0.2 * jnp.clip(jax.random.normal(subkeys[4], extent), -3.0, 3.0)
    sediment = water * jax.random.uniform(subkeys[3], extent, minval=0.0, maxval=0.06)
    friction = jnp.exp(jax.random.uniform(subkeys[5], extent, minval=math.log(0.01), maxval=math.log(0.1)))
    return jnp.stack([water, flow_x, flow_y, sediment, bed_level, friction], 1).astype(jnp.float32)


def draw_neighbors(key, part):
    patch_count = PATCHES
    bit_count = patch_count.bit_length() - 1
    across_bits = (bit_count + 1) // 2
    upward_bits = bit_count - across_bits
    grid_across = 1 << across_bits
    grid_upward = 1 << upward_bits
    subkeys = jax.random.split(key, 2)
    lower_pattern = jnp.array([0] * (across_bits - 1) + [1] * upward_bits, dtype=jnp.int32)
    ordering = jnp.concatenate([jax.random.permutation(subkeys[0], lower_pattern), jnp.zeros((1,), jnp.int32)])
    is_across = (ordering == 0).astype(jnp.int32)
    across_rank = jnp.cumsum(is_across) - is_across
    upward_rank = jnp.cumsum(1 - is_across) - (1 - is_across)
    curve_index = jnp.arange(patch_count, dtype=jnp.int32)
    column = jnp.zeros(patch_count, jnp.int32)
    row_place = jnp.zeros(patch_count, jnp.int32)
    for level in range(bit_count):
        digit = jnp.right_shift(curve_index, level) & 1
        column = column + jnp.where(ordering[level] == 0, jnp.left_shift(digit, across_rank[level]), 0)
        row_place = row_place + jnp.where(ordering[level] == 1, jnp.left_shift(digit, upward_rank[level]), 0)
    top_digit = jnp.right_shift(curve_index, bit_count - 1) & 1
    column = jnp.where(top_digit == 1, jnp.bitwise_xor(column, grid_across // 2 - 1), column)
    flipping = jax.random.randint(subkeys[1], (2,), 0, 2)
    column = jnp.where(flipping[0] == 1, grid_across - 1 - column, column)
    row_place = jnp.where(flipping[1] == 1, grid_upward - 1 - row_place, row_place)
    position = row_place * grid_across + column
    lookup = jnp.zeros(patch_count, jnp.int32).at[position].set(curve_index)
    west = jnp.where(column > 0, lookup[jnp.maximum(position - 1, 0)], -1)
    east = jnp.where(column < grid_across - 1, lookup[jnp.minimum(position + 1, patch_count - 1)], -1)
    south = jnp.where(row_place > 0, lookup[jnp.maximum(position - grid_across, 0)], -1)
    north = jnp.where(row_place < grid_upward - 1, lookup[jnp.minimum(position + grid_across, patch_count - 1)], -1)
    return jnp.stack([west, east, south, north], 1).astype(jnp.int32)


def draw_migration(key, part):
    scores = jax.random.randint(key, (OWNERS, P_DEV), 0, 1 << 20) * P_DEV + jnp.arange(P_DEV, dtype=jnp.int32)[None, :]
    ordering = jnp.argsort(scores, axis=1)
    return ordering[:, :MIG].astype(jnp.int32)


def with_ends(values, rng, low, largest):
    shape = values.shape
    spot = [jax.random.randint(jax.random.fold_in(rng, axis), (), 0, shape[axis]) for axis in range(len(shape))]
    values = values.at[tuple(spot)].set(low)
    longest = shape.index(max(shape))
    spot[longest] = (spot[longest] + 1) % shape[longest]
    return values.at[tuple(spot)].set(largest)


def setup_inputs(seed: int = 0) -> dict:
    splits = jax.random.split(jax.random.key(seed), 5)
    fields = draw_fields(jax.random.fold_in(splits[4], 71), 0)
    wet_mask = with_ends((jax.random.randint(splits[1], (PATCHES, PS, PS), 0, 4) < 3).astype(jnp.int32), jax.random.fold_in(splits[1], 1), 0, 1)
    neighbors = draw_neighbors(jax.random.fold_in(splits[4], 71), 0)
    migration = draw_migration(jax.random.fold_in(splits[4], 71), 0)
    return dict(fields=fields, wet_mask=wet_mask, neighbors=neighbors, migration=migration)


GRAVITY = 9.81
TIME_STEP = 0.04
DRY_EPS = 0.01
CAPACITY = 0.02
EROSION = 0.5
SETTLING = 0.2
POROSITY = 0.4

def face_flux(left_depth, left_normal, left_along, left_sed, right_depth, right_normal, right_along, right_sed):
    left_inverse = left_depth / (left_depth * left_depth + DRY_EPS)
    right_inverse = right_depth / (right_depth * right_depth + DRY_EPS)
    left_speed = left_normal * left_inverse
    right_speed = right_normal * right_inverse
    left_cross = left_along * left_inverse
    right_cross = right_along * right_inverse
    left_conc = left_sed * left_inverse
    right_conc = right_sed * right_inverse
    left_root = jnp.sqrt(jnp.maximum(left_depth, 0.0) + 0.01)
    right_root = jnp.sqrt(jnp.maximum(right_depth, 0.0) + 0.01)
    weights = left_root + right_root
    mean_speed = (left_root * left_speed + right_root * right_speed) / weights
    mean_cross = (left_root * left_cross + right_root * right_cross) / weights
    mean_conc = (left_root * left_conc + right_root * right_conc) / weights
    celerity = jnp.sqrt(GRAVITY * 0.5 * (jnp.maximum(left_depth, 0.0) + jnp.maximum(right_depth, 0.0))) + 0.1
    jump_depth = right_depth - left_depth
    jump_normal = right_normal - left_normal
    jump_along = right_along - left_along
    jump_sed = right_sed - left_sed
    slow_wave = ((mean_speed + celerity) * jump_depth - jump_normal) / (2.0 * celerity)
    fast_wave = (jump_normal - (mean_speed - celerity) * jump_depth) / (2.0 * celerity)
    shear_wave = jump_along - mean_cross * jump_depth
    sed_wave = jump_sed - mean_conc * jump_depth
    slow_part = jnp.abs(mean_speed - celerity) * slow_wave
    fast_part = jnp.abs(mean_speed + celerity) * fast_wave
    middle = jnp.abs(mean_speed)
    both_parts = slow_part + fast_part
    flux_depth = 0.5 * (left_normal + right_normal) - 0.5 * both_parts
    flux_normal = 0.5 * (left_normal * left_speed + 0.5 * GRAVITY * left_depth * left_depth + right_normal * right_speed + 0.5 * GRAVITY * right_depth * right_depth) - 0.5 * (slow_part * (mean_speed - celerity) + fast_part * (mean_speed + celerity))
    flux_along = 0.5 * (left_normal * left_cross + right_normal * right_cross) - 0.5 * (both_parts * mean_cross + middle * shear_wave)
    flux_sed = 0.5 * (left_normal * left_conc + right_normal * right_conc) - 0.5 * (both_parts * mean_conc + middle * sed_wave)
    return (flux_depth, flux_normal, flux_along, flux_sed)

def inner_part(field):
    return field[..., 1:-1, 1:-1]

def x_change(flux):
    return flux[..., 1:] - flux[..., :-1]

def y_change(flux):
    return flux[..., 1:, :] - flux[..., :-1, :]

def advance(extended):
    water = extended[..., 0, :, :]
    flow_x = extended[..., 1, :, :]
    flow_y = extended[..., 2, :, :]
    sediment = extended[..., 3, :, :]
    bed_level = extended[..., 4, :, :]
    friction = extended[..., 5, :, :]
    x_flux = face_flux(water[..., 1:-1, :-1], flow_x[..., 1:-1, :-1], flow_y[..., 1:-1, :-1], sediment[..., 1:-1, :-1], water[..., 1:-1, 1:], flow_x[..., 1:-1, 1:], flow_y[..., 1:-1, 1:], sediment[..., 1:-1, 1:])
    y_flux = face_flux(water[..., :-1, 1:-1], flow_y[..., :-1, 1:-1], flow_x[..., :-1, 1:-1], sediment[..., :-1, 1:-1], water[..., 1:, 1:-1], flow_y[..., 1:, 1:-1], flow_x[..., 1:, 1:-1], sediment[..., 1:, 1:-1])
    old_water = inner_part(water)
    new_water = old_water - TIME_STEP * (x_change(x_flux[0]) + y_change(y_flux[0]))
    new_x = inner_part(flow_x) - TIME_STEP * (x_change(x_flux[1]) + y_change(y_flux[2])) - TIME_STEP * GRAVITY * old_water * 0.5 * (bed_level[..., 1:-1, 2:] - bed_level[..., 1:-1, :-2])
    new_y = inner_part(flow_y) - TIME_STEP * (x_change(x_flux[2]) + y_change(y_flux[1])) - TIME_STEP * GRAVITY * old_water * 0.5 * (bed_level[..., 2:, 1:-1] - bed_level[..., :-2, 1:-1])
    new_sed = inner_part(sediment) - TIME_STEP * (x_change(x_flux[3]) + y_change(y_flux[3]))
    inverse = new_water / (new_water * new_water + DRY_EPS)
    speed = jnp.sqrt((new_x * inverse) ** 2 + (new_y * inverse) ** 2)
    inner_friction = inner_part(friction)
    factor = 1.0 / (1.0 + TIME_STEP * inner_friction * speed / (jnp.maximum(new_water, 0.0) + 0.1))
    new_x = new_x * factor
    new_y = new_y * factor
    concentration = new_sed * inverse
    net_rate = EROSION * jnp.maximum(CAPACITY * speed * speed - concentration, 0.0) - SETTLING * concentration
    new_sed = new_sed + TIME_STEP * net_rate
    new_bed = inner_part(bed_level) - TIME_STEP * net_rate / (1.0 - POROSITY)
    return jnp.stack([new_water, new_x, new_y, new_sed, new_bed, inner_friction], -3)

def pick_from(source, which, fallback):
    usable = (which >= 0)[:, None, None, None]
    return jnp.where(usable, source[jnp.maximum(which, 0)], fallback)

def extend(patches, neighbors):
    extent = patches.shape[-1]
    west = pick_from(patches[..., extent - 2:], neighbors[:, 0], jnp.repeat(patches[..., :1], 2, -1))
    east = pick_from(patches[..., :2], neighbors[:, 1], jnp.repeat(patches[..., -1:], 2, -1))
    widened = jnp.concatenate([west, patches, east], -1)
    south = pick_from(widened[..., extent - 2:extent, :], neighbors[:, 2], jnp.repeat(widened[..., :1, :], 2, -2))
    north = pick_from(widened[..., :2, :], neighbors[:, 3], jnp.repeat(widened[..., -1:, :], 2, -2))
    return jnp.concatenate([south, widened, north], -2)

def two_steps(patch_block):
    return advance(advance(patch_block))

def run_round(patches, neighbors):
    extended = extend(patches, neighbors)
    side = extended.shape[-1]
    blocks = extended.reshape(-1, P_DEV, 6, side, side)
    stepped = lax.map(two_steps, blocks)
    return stepped.reshape(-1, 6, side - 4, side - 4)

def reference(fields, wet_mask, neighbors, migration):
    wetness = wet_mask.astype(jnp.float32)
    unity = jnp.ones_like(wetness)
    scaling = jnp.stack([wetness, wetness, wetness, wetness, unity, unity], 1)
    patches = fields * scaling
    patches = run_round(patches, neighbors)
    patches = run_round(patches, neighbors)
    owner_count = migration.shape[0]
    layout = jnp.arange(owner_count * P_DEV, dtype=jnp.int32).reshape(owner_count, P_DEV)
    previous = (jnp.arange(owner_count, dtype=jnp.int32) - 1) % owner_count
    incoming = previous[:, None] * P_DEV + jnp.roll(migration, 1, axis=0)
    layout = layout.at[jnp.arange(owner_count, dtype=jnp.int32)[:, None], migration].set(incoming)
    return patches[layout.reshape(-1)]
```

```python
import functools

import jax
import jax.numpy as jnp
from jax import lax
from jax.experimental import pallas as pl
from jax.experimental.pallas import tpu as pltpu
from jax.sharding import PartitionSpec as P

GRAVITY = 9.81
TIME_STEP = 0.04
DRY_EPS = 0.01
CAPACITY = 0.02
EROSION = 0.5
SETTLING = 0.2
POROSITY = 0.4

LANES = 128
SUB = 8
WEST, EAST, SOUTH, NORTH = range(4)
BED_TILE, FRICTION_TILE, TILES = 4, 5, 6
VMEM_LIMIT = 48 * 1024 * 1024
VMEM = pl.BlockSpec(memory_space=pltpu.VMEM)
SMEM = pl.BlockSpec(memory_space=pltpu.SMEM)
ANY = pl.BlockSpec(memory_space=pl.ANY)


def lane_index():
    return lax.broadcasted_iota(jnp.int32, (SUB, LANES), 1)


def row_index():
    return lax.broadcasted_iota(jnp.int32, (SUB, LANES), 0)


def lane_roll(value, shift):
    shift = shift % LANES
    return value if shift == 0 else pltpu.roll(value, shift, 1)


def row_roll(value, shift):
    shift = shift % SUB
    return value if shift == 0 else pltpu.roll(value, shift, 0)


def everywhere(flag):
    return jnp.full((SUB, LANES), flag.astype(jnp.int32)) > 0


def root_of(value):
    return value * lax.rsqrt(jnp.maximum(value, 1e-30))


def cell_terms(h, qx, qy, m):
    inverse = h / (h * h + DRY_EPS)
    wet = jnp.maximum(h, 0.0)
    return (h, qx, qy, m, qx * inverse, qy * inverse, m * inverse, root_of(wet + 0.01))


def doubled_flux(left, right):
    h0, n0, t0, m0, u0, w0, s0, r0 = left
    h1, n1, t1, m1, u1, w1, s1, r1 = right
    scale = 1.0 / (r0 + r1)
    part0 = r0 * scale
    part1 = r1 * scale
    mean_u = part0 * u0 + part1 * u1
    mean_w = part0 * w0 + part1 * w1
    mean_s = part0 * s0 + part1 * s1
    celerity = root_of((0.5 * GRAVITY) * (jnp.maximum(h0, 0.0) + jnp.maximum(h1, 0.0))) + 0.1
    half = 0.5 / celerity
    dh = h1 - h0
    dn = n1 - n0
    plus = mean_u + celerity
    minus = mean_u - celerity
    p1 = jnp.abs(minus) * ((plus * dh - dn) * half)
    p3 = jnp.abs(plus) * ((dn - minus * dh) * half)
    both = p1 + p3
    middle = jnp.abs(mean_u)
    return (
        n0 + n1 - both,
        n0 * u0 + n1 * u1 + (0.5 * GRAVITY) * (h0 * h0 + h1 * h1) - (p1 * minus + p3 * plus),
        n0 * w0 + n1 * w1 - (both * mean_w + middle * (t1 - t0 - mean_w * dh)),
        n0 * s0 + n1 * s1 - (both * mean_s + middle * (m1 - m0 - mean_s * dh)),
    )


def swapped(cell):
    h, qx, qy, m, u, v, s, r = cell
    return (h, qy, qx, m, v, u, s, r)


def advance_rows(load, store, count, unroll):
    rows = row_index()
    first, last = rows == 0, rows == SUB - 1

    def upper(now, after):
        return row_roll(jnp.where(first, after, now), -1)

    def lower(before_rolled, rolled):
        return jnp.where(first, before_rolled, rolled)

    def fetch(k):
        return cell_terms(load(0, k), load(1, k), load(2, k), load(3, k)) + (load(4, k),)

    def body(k, carry):
        now, flux_before, bed_before = carry
        after = fetch(jnp.minimum(k + 1, count - 1)) if count > 1 else now
        cell, bed = now[:8], now[8]
        up = tuple(upper(a, b) for a, b in zip(cell, after[:8]))
        y_flux = doubled_flux(swapped(cell), swapped(up))
        y_rolled = tuple(row_roll(f, 1) for f in y_flux)
        dy = tuple(f - lower(b, r) for f, b, r in zip(y_flux, flux_before, y_rolled))
        west = tuple(lane_roll(a, 1) for a in cell)
        x_flux = doubled_flux(west, cell)
        dx = tuple(lane_roll(f, -1) - f for f in x_flux)
        bed_rolled = row_roll(bed, 1)
        bed_y = upper(bed, after[8]) - lower(bed_before, bed_rolled)
        bed_x = lane_roll(bed, -1) - lane_roll(bed, 1)
        h, qx, qy, m = cell[:4]
        friction = load(5, k)
        step = 0.5 * TIME_STEP
        slope = (step * GRAVITY) * h
        new_h = h - step * (dx[0] + dy[0])
        new_x = qx - step * (dx[1] + dy[2]) - slope * bed_x
        new_y = qy - step * (dx[2] + dy[1]) - slope * bed_y
        new_m = m - step * (dx[3] + dy[3])
        inverse = new_h / (new_h * new_h + DRY_EPS)
        speed_x = new_x * inverse
        speed_y = new_y * inverse
        square = speed_x * speed_x + speed_y * speed_y
        speed = root_of(square)
        depth = jnp.maximum(new_h, 0.0) + 0.1
        factor = depth / (depth + TIME_STEP * friction * speed)
        conc = new_m * inverse
        net = EROSION * jnp.maximum(CAPACITY * square - conc, 0.0) - SETTLING * conc
        store(0, k, new_h)
        store(1, k, new_x * factor)
        store(2, k, new_y * factor)
        store(3, k, new_m + TIME_STEP * net)
        store(4, k, bed - (TIME_STEP / (1.0 - POROSITY)) * net)
        return after, y_rolled, bed_rolled

    zero = jnp.zeros((SUB, LANES), jnp.float32)
    start = (fetch(0), (zero,) * 4, zero)
    if count == 1:
        body(0, start)
    else:
        lax.fori_loop(0, count, body, start, unroll=unroll)


def chunk(k):
    return pl.ds(pl.multiple_of(k * SUB, SUB), SUB)


def pack_frames(patches, frames, turned):
    per_dev, _, extent, _ = patches.shape
    lanes = lane_index()

    def columns(k, _):
        total = jnp.zeros((SUB, LANES), jnp.float32)
        for p in range(per_dev):
            for f in range(6):
                value = patches[p, f, chunk(k), :]
                base = p * 32
                if f < 4:
                    spots = ((base + 2 * f, 2, 0), (base + 8 + 2 * f, 2, LANES - 2))
                elif f == 4:
                    spots = ((base + 16, 2, 0), (base + 18, 2, LANES - 2))
                else:
                    spots = ((base + 24, 1, 0), (base + 25, 1, LANES - 1))
                for spot, width, origin in spots:
                    inside = (lanes >= spot) & (lanes < spot + width)
                    total = jnp.where(inside, lane_roll(value, spot - origin), total)
        turned[chunk(k), :] = total
        return 0

    lax.fori_loop(0, extent // SUB, columns, 0)
    turned[...] = turned[...].T
    rows = row_index()
    low, high = slice(0, SUB), slice(extent - SUB, extent)
    for p in range(per_dev):
        base = p * 32
        frames[p, WEST] = turned[base : base + 8]
        frames[p, EAST] = turned[base + 8 : base + 16]
        south = north = jnp.zeros((SUB, LANES), jnp.float32)
        for f in range(4):
            inside = (rows >= 2 * f) & (rows < 2 * f + 2)
            south = jnp.where(inside, row_roll(patches[p, f, low, :], 2 * f), south)
            north = jnp.where(inside, row_roll(patches[p, f, high, :], 2 * f + 2), north)
        frames[p, SOUTH] = south
        frames[p, NORTH] = north
        bed = turned[base + 16 : base + 24]
        bed = jnp.where((rows == 4) | (rows == 5), row_roll(patches[p, 4, low, :], 4), bed)
        bed = jnp.where(rows >= 6, patches[p, 4, high, :], bed)
        frames[p, BED_TILE] = bed
        rough = turned[base + 24 : base + 32]
        rough = jnp.where(rows == 2, row_roll(patches[p, 5, low, :], 2), rough)
        rough = jnp.where(rows == 3, row_roll(patches[p, 5, high, :], 4), rough)
        frames[p, FRICTION_TILE] = rough


def begin_kernel(fields, mask, started, frames, turned):
    for p in range(fields.shape[0]):
        wet = mask[p].astype(jnp.float32)
        for f in range(6):
            started[p, f] = fields[p, f] * wet if f < 4 else fields[p, f]
    pack_frames(started, frames, turned)


def begin(fields, mask):
    per_dev = fields.shape[0]
    return pl.pallas_call(
        begin_kernel,
        out_shape=(
            jax.ShapeDtypeStruct(fields.shape, jnp.float32),
            jax.ShapeDtypeStruct((per_dev, TILES, SUB, LANES), jnp.float32),
        ),
        in_specs=[VMEM, VMEM],
        out_specs=(VMEM, VMEM),
        scratch_shapes=[pltpu.VMEM((LANES, LANES), jnp.float32)],
        compiler_params=pltpu.CompilerParams(vmem_limit_bytes=VMEM_LIMIT),
    )(fields, mask)


def gather_kernel(count, mine, pool, own_sem, send_sem, recv_sem):
    per_dev = mine.shape[0]
    length = count // 8
    me = lax.axis_index("curve")
    core, x, y, z = me % 2, (me // 2) % 2, (me // 4) % 2, me // 8
    other_core = me + 1 - 2 * core
    other_x = me + 2 - 4 * x
    other_y = me + 4 - 8 * y
    across = 6 - 4 * x - 8 * y
    has_up, has_down = z < length - 1, z > 0
    above = jnp.where(has_up, me + 8, me - 8)
    below = jnp.where(has_down, me - 8, me + 8)

    barrier = pltpu.get_barrier_semaphore()

    def greet(device):
        pl.semaphore_signal(
            barrier, inc=1, device_id=(device,), device_id_type=pl.DeviceIdType.MESH
        )

    for device in (other_core, other_x, other_y):
        greet(device)
    pl.when(has_up)(lambda: greet(above))
    pl.when(has_down)(lambda: greet(below))
    pl.semaphore_wait(barrier, 3 + has_up.astype(jnp.int32) + has_down.astype(jnp.int32))

    def place(block):
        return pool.at[pl.ds(block * per_dev, per_dev)]

    sends = []

    def copy_of(block, device, slot, own=False):
        return pltpu.make_async_remote_copy(
            src_ref=mine if own else place(block),
            dst_ref=place(block),
            send_sem=send_sem.at[slot],
            recv_sem=recv_sem.at[block],
            device_id=(device,),
            device_id_type=pl.DeviceIdType.MESH,
        )

    def send(block, device, own=False, when=None):
        slot = len(sends)
        sends.append((block, device, own, when))
        copy = copy_of(block, device, slot, own)
        if when is None:
            copy.start()
        else:
            pl.when(when)(copy.start)

    def arrive(block, when=None):
        copy = copy_of(block, other_core, 0)
        if when is None:
            copy.wait_recv()
        else:
            pl.when(when)(copy.wait_recv)

    own_copy = pltpu.make_async_copy(mine, place(me), own_sem)
    own_copy.start()
    send(me, above, True, has_up)
    send(me, below, True, has_down)
    send(me, other_x, True)
    send(me, other_y, True)
    send(me, other_core, True)

    def sideways(level, when):
        x_block = level * 8 + other_x % 8
        y_block = level * 8 + other_y % 8
        even = level % 2 == 0
        odd = level % 2 == 1
        arrive(x_block, when)
        send(x_block, other_y, when=even if when is None else even & when)
        send(x_block, other_core, when=when)
        arrive(y_block, when)
        send(y_block, other_x, when=odd if when is None else odd & when)
        send(y_block, other_core, when=when)

    def diagonal(level, when):
        block = level * 8 + (me + across) % 8
        arrive(block, when)
        send(block, other_core, when=when)

    levels = [(z, None)]
    for distance in range(1, length):
        levels += [(z - distance, z >= distance), (z + distance, z + distance < length)]
    done = 0
    for distance in range(1, length):
        for sign, there in ((-1, z >= distance), (1, z + distance < length)):
            level = z + sign * distance
            block = me + 8 * sign * distance
            arrive(block, there)
            if distance < length - 1:
                if sign < 0:
                    send(block, above, when=there & has_up)
                else:
                    send(block, below, when=there & has_down)
            send(block, other_x, when=there)
            send(block, other_y, when=there)
            send(block, other_core, when=there)
        while done < 2 * distance - 1:
            sideways(*levels[done])
            done += 1
    while done < len(levels):
        sideways(*levels[done])
        done += 1
    for level in levels:
        diagonal(*level)
    for column in range(4):
        base = (other_core % 2) + (column % 2) * 2 + (column // 2) * 4
        for level in range(length):
            arrive(level * 8 + base)
    own_copy.wait()
    for slot, (block, device, own, when) in enumerate(sends):
        copy = copy_of(block, device, slot, own)
        if when is None:
            copy.wait_send()
        else:
            pl.when(when)(copy.wait_send)


def gather_frames(frames, count, collective_id):
    per_dev = frames.shape[0]
    return pl.pallas_call(
        functools.partial(gather_kernel, count),
        out_shape=jax.ShapeDtypeStruct((count * per_dev,) + frames.shape[1:], jnp.float32),
        in_specs=[ANY],
        out_specs=ANY,
        scratch_shapes=[
            pltpu.SemaphoreType.DMA,
            pltpu.SemaphoreType.DMA((5 * count,)),
            pltpu.SemaphoreType.DMA((count,)),
        ],
        compiler_params=pltpu.CompilerParams(collective_id=collective_id, has_side_effects=True),
    )(frames)


def step_kernel(
    count, moved, with_frames, device, neighbors, migration, patches, pool, *refs
):
    if with_frames:
        ended, frames, middle, strip_a, strip_b, rows_a, rows_b, turned, halo = refs
    else:
        ended, middle, strip_a, strip_b, rows_a, rows_b, turned, halo = refs
    per_dev, _, extent, _ = patches.shape
    chunks = extent // SUB
    moves = migration.shape[1]
    owner = device[0]
    lanes, rows = lane_index(), row_index()

    def ring(value):
        return jnp.where(value < 0, value + count, jnp.where(value >= count, value - count, value))

    def patch_in(slot):
        before = ring(owner - 1)
        result = owner * per_dev + slot
        for k in range(moves):
            result = jnp.where(
                migration[owner, k] == slot, before * per_dev + migration[before, k], result
            )
        return result

    def position(patch):
        if not moved:
            return patch
        home = patch // per_dev
        slot = patch - home * per_dev
        after = ring(home + 1)
        result = patch
        for k in range(moves):
            result = jnp.where(
                migration[home, k] == slot, after * per_dev + migration[after, k], result
            )
        return result

    opposite = {WEST: EAST, EAST: WEST, SOUTH: NORTH, NORTH: SOUTH}

    def repaired(tile, side, missing):
        if side in (WEST, SOUTH):
            return jnp.where(everywhere(missing) & (rows % 2 == 1), row_roll(tile, 1), tile)
        return jnp.where(everywhere(missing) & (rows % 2 == 0), row_roll(tile, -1), tile)

    def edge_tiles(patch, side):
        beyond = neighbors[patch, side]
        missing = beyond < 0
        source = position(jnp.where(missing, patch, beyond))
        edge = jnp.where(missing, side, opposite[side])
        flow = repaired(pool[source, edge], side, missing)
        bed = pool[source, BED_TILE]
        bed = jnp.where(everywhere(missing), row_roll(bed, -2 * side), row_roll(bed, -2 * opposite[side]))
        bed = repaired(bed, side, missing)
        rough = pool[source, FRICTION_TILE]
        rough = jnp.where(everywhere(missing), row_roll(rough, -side), row_roll(rough, -opposite[side]))
        return flow, bed, rough

    def by_field(flow, bed, rough, spot, near):
        return [row_roll(flow, spot - 2 * f) for f in range(4)] + [
            row_roll(bed, spot),
            row_roll(rough, near),
        ]

    for p in range(per_dev):
        patch = patch_in(p)
        for side, spot, near in ((WEST, 0, 1), (EAST, 6, 6)):
            group = 2 * p + side
            for f, tile in enumerate(by_field(*edge_tiles(patch, side), spot, near)):
                turned[f, group * SUB : (group + 1) * SUB] = tile
        for end, side, spot, near in ((0, SOUTH, 6, 7), (1, NORTH, 0, 0)):
            for f, tile in enumerate(by_field(*edge_tiles(patch, side), spot, near)):
                halo[p, end, f] = tile

    for f in range(6):
        turned[f] = turned[f].T

    group_lane = lanes % SUB
    odd_group = (lanes // SUB) % 2
    from_halo = ((odd_group == 0) & (group_lane < 2)) | ((odd_group == 1) & (group_lane >= 6))

    def lay_strip(f, take):
        total = jnp.zeros((SUB, LANES), jnp.float32)
        for p in range(per_dev):
            value = take(p)
            for side, shift in ((WEST, 2), (EAST, 6)):
                group = 2 * p + side
                total = jnp.where(
                    lanes // SUB == group, lane_roll(value, group * SUB + shift), total
                )
        return total

    def fill_strip(k, _):
        for f in range(6):
            own = lay_strip(f, lambda p: patches[p, f, chunk(k), :])
            strip_a[f, chunk(k + 1), :] = jnp.where(from_halo, turned[f, chunk(k), :], own)
        return 0

    lax.fori_loop(0, chunks, fill_strip, 0)

    for end, side, row, line in ((0, SOUTH, 7, 1), (1, NORTH, 0, 0)):
        place = slice(0, SUB) if end == 0 else slice((chunks + 1) * SUB, (chunks + 2) * SUB)
        corner = [lay_strip(f, lambda p: halo[p, end, f]) for f in range(6)]
        for p in range(per_dev):
            patch = patch_in(p)
            beyond = neighbors[patch, side]
            missing = beyond < 0
            base = jnp.where(missing, patch, beyond)
            edge = jnp.where(missing, side, opposite[side])
            for across, spot, inner, outer in ((WEST, 1, 0, LANES - 1), (EAST, 6, LANES - 1, 0)):
                aside = neighbors[base, across]
                alone = aside < 0
                source = position(jnp.where(alone, base, aside))
                lane = (2 * p + across) * SUB + spot
                flow = repaired(pool[source, edge], side, missing)
                bed = pool[source, BED_TILE]
                bed = jnp.where(
                    everywhere(missing), row_roll(bed, -2 * side), row_roll(bed, -2 * opposite[side])
                )
                bed = repaired(bed, side, missing)
                flow = jnp.where(everywhere(alone), lane_roll(flow, lane - inner), lane_roll(flow, lane - outer))
                bed = jnp.where(everywhere(alone), lane_roll(bed, lane - inner), lane_roll(bed, lane - outer))
                here = (lanes == lane) & (rows == row)
                for f in range(4):
                    corner[f] = jnp.where(here, row_roll(flow, row - 2 * f - line), corner[f])
                corner[4] = jnp.where(here, row_roll(bed, row - line), corner[4])
        for f in range(6):
            strip_a[f, place, :] = corner[f]

    for p in range(per_dev):
        for f in range(6):
            low = patches[p, f, 0:SUB, :]
            high = patches[p, f, extent - SUB : extent, :]
            rows_a[2 * p, f] = jnp.where(
                rows < 2, row_roll(halo[p, 0, f], 2), row_roll(low, 2)
            )
            rows_a[2 * p + 1, f] = jnp.where(
                rows >= 6, row_roll(halo[p, 1, f], 6), row_roll(high, -2)
            )

    def run(source, rough, target, count, unroll):
        def load(f, k):
            return (rough if f == 5 else source)[f, chunk(k), :]

        def store(f, k, value):
            target[f, chunk(k), :] = value

        advance_rows(load, store, count, unroll)

    run(strip_a, strip_a, strip_b, chunks + 2, 2)
    run(strip_b, strip_a, strip_a, chunks + 2, 2)

    def row_strip(i, _):
        def load_a(f, k):
            return rows_a[i, f]

        def store_b(f, k, value):
            rows_b[i, f] = value

        advance_rows(load_a, store_b, 1, 1)

        def load_b(f, k):
            return rows_a[i, f] if f == 5 else rows_b[i, f]

        def store_a(f, k, value):
            rows_a[i, f] = value

        advance_rows(load_b, store_a, 1, 1)
        return 0

    lax.fori_loop(0, 2 * per_dev, row_strip, 0, unroll=2)

    def main_patch(p, _):
        start, end = patches.at[p], ended.at[p]
        run(start, start, middle, chunks, 2)
        run(middle, start, end, chunks, 2)
        return 0

    lax.fori_loop(0, per_dev, main_patch, 0)

    for p in range(per_dev):
        for f in range(5):
            low = ended[p, f, 0:SUB, :]
            ended[p, f, 0:SUB, :] = jnp.where(rows < 2, row_roll(rows_a[2 * p, f], -2), low)
            high = ended[p, f, extent - SUB : extent, :]
            ended[p, f, extent - SUB : extent, :] = jnp.where(
                rows >= 6, row_roll(rows_a[2 * p + 1, f], 2), high
            )

    def merge(k, _):
        for f in range(5):
            strip = strip_a[f, chunk(k + 1), :]
            for p in range(per_dev):
                west = lane_roll(strip, -(2 * p * SUB + 2))
                east = lane_roll(strip, -6 - (2 * p + 1) * SUB)
                value = ended[p, f, chunk(k), :]
                value = jnp.where(lanes < 2, west, value)
                ended[p, f, chunk(k), :] = jnp.where(lanes >= LANES - 2, east, value)
        for p in range(per_dev):
            ended[p, 5, chunk(k), :] = patches[p, 5, chunk(k), :]
        return 0

    lax.fori_loop(0, chunks, merge, 0)
    if with_frames:
        pack_frames(ended, frames, turned.at[0])


def two_steps(device, neighbors, migration, patches, pool, count, moved, with_frames):
    per_dev, _, extent, _ = patches.shape
    out_shape = [jax.ShapeDtypeStruct(patches.shape, jnp.float32)]
    if with_frames:
        out_shape.append(jax.ShapeDtypeStruct((per_dev, TILES, SUB, LANES), jnp.float32))
    return pl.pallas_call(
        functools.partial(step_kernel, count, moved, with_frames),
        out_shape=tuple(out_shape),
        in_specs=[SMEM, SMEM, SMEM, VMEM, VMEM],
        out_specs=(VMEM,) * len(out_shape),
        scratch_shapes=[
            pltpu.VMEM((6, extent, LANES), jnp.float32),
            pltpu.VMEM((6, extent + 2 * SUB, LANES), jnp.float32),
            pltpu.VMEM((6, extent + 2 * SUB, LANES), jnp.float32),
            pltpu.VMEM((2 * per_dev, 6, SUB, LANES), jnp.float32),
            pltpu.VMEM((2 * per_dev, 6, SUB, LANES), jnp.float32),
            pltpu.VMEM((6, LANES, LANES), jnp.float32),
            pltpu.VMEM((per_dev, 2, 6, SUB, LANES), jnp.float32),
        ],
        compiler_params=pltpu.CompilerParams(vmem_limit_bytes=VMEM_LIMIT),
    )(device, neighbors, migration, patches, pool)


def shards(fields, wet_mask, neighbors, migration):
    device = lax.axis_index("curve")
    count = lax.axis_size("curve")
    started, frames = begin(fields, wet_mask)
    leaving = lax.dynamic_slice_in_dim(migration, device, 1, 0)[0]
    route = [(source, (source + 1) % count) for source in range(count)]
    arriving = lax.ppermute(started[leaving], "curve", route)
    pool = gather_frames(frames, count, 0)
    patches = started.at[leaving].set(arriving)
    spot = device.astype(jnp.int32).reshape(1)
    halfway, frames = two_steps(spot, neighbors, migration, patches, pool, count, False, True)
    pool = gather_frames(frames, count, 0)
    (ended,) = two_steps(spot, neighbors, migration, halfway, pool, count, True, False)
    return ended


def solution(mesh):
    placed = (P("curve", None, None, None), P("curve", None, None), P(), P())
    return jax.shard_map(
        shards, mesh=mesh, in_specs=placed, out_specs=P("curve", None, None, None), check_vma=False
    )
```

```python
import functools

import jax
import jax.numpy as jnp
from jax import lax
from jax.experimental import pallas as pl
from jax.experimental.pallas import tpu as pltpu
from jax.sharding import PartitionSpec as P

GRAVITY = 9.81
TIME_STEP = 0.04
DRY_EPS = 0.01
CAPACITY = 0.02
EROSION = 0.5
SETTLING = 0.2
POROSITY = 0.4

LANES = 128
SUB = 8
WEST, EAST, SOUTH, NORTH = range(4)
BED_TILE, FRICTION_TILE, TILES = 4, 5, 6
VMEM_LIMIT = 48 * 1024 * 1024
VMEM = pl.BlockSpec(memory_space=pltpu.VMEM)
SMEM = pl.BlockSpec(memory_space=pltpu.SMEM)
ANY = pl.BlockSpec(memory_space=pl.ANY)


def lane_index():
    return lax.broadcasted_iota(jnp.int32, (SUB, LANES), 1)


def row_index():
    return lax.broadcasted_iota(jnp.int32, (SUB, LANES), 0)


def lane_roll(value, shift):
    shift = shift % LANES
    return value if shift == 0 else pltpu.roll(value, shift, 1)


def row_roll(value, shift):
    shift = shift % SUB
    return value if shift == 0 else pltpu.roll(value, shift, 0)


def everywhere(flag):
    return jnp.full((SUB, LANES), flag.astype(jnp.int32)) > 0


def root_of(value):
    return value * lax.rsqrt(jnp.maximum(value, 1e-30))


def cell_terms(h, qx, qy, m):
    inverse = h / (h * h + DRY_EPS)
    wet = jnp.maximum(h, 0.0)
    return (h, qx, qy, m, qx * inverse, qy * inverse, m * inverse, root_of(wet + 0.01))


def doubled_flux(left, right):
    h0, n0, t0, m0, u0, w0, s0, r0 = left
    h1, n1, t1, m1, u1, w1, s1, r1 = right
    scale = 1.0 / (r0 + r1)
    part0 = r0 * scale
    part1 = r1 * scale
    mean_u = part0 * u0 + part1 * u1
    mean_w = part0 * w0 + part1 * w1
    mean_s = part0 * s0 + part1 * s1
    celerity = root_of((0.5 * GRAVITY) * (jnp.maximum(h0, 0.0) + jnp.maximum(h1, 0.0))) + 0.1
    half = 0.5 / celerity
    dh = h1 - h0
    dn = n1 - n0
    plus = mean_u + celerity
    minus = mean_u - celerity
    p1 = jnp.abs(minus) * ((plus * dh - dn) * half)
    p3 = jnp.abs(plus) * ((dn - minus * dh) * half)
    both = p1 + p3
    middle = jnp.abs(mean_u)
    return (
        n0 + n1 - both,
        n0 * u0 + n1 * u1 + (0.5 * GRAVITY) * (h0 * h0 + h1 * h1) - (p1 * minus + p3 * plus),
        n0 * w0 + n1 * w1 - (both * mean_w + middle * (t1 - t0 - mean_w * dh)),
        n0 * s0 + n1 * s1 - (both * mean_s + middle * (m1 - m0 - mean_s * dh)),
    )


def swapped(cell):
    h, qx, qy, m, u, v, s, r = cell
    return (h, qy, qx, m, v, u, s, r)


def advance_rows(load, store, count, unroll, slices=1, pause=None):
    rows = row_index()
    first, last = rows == 0, rows == SUB - 1

    def upper(now, after):
        return row_roll(jnp.where(first, after, now), -1)

    def lower(before_rolled, rolled):
        return jnp.where(first, before_rolled, rolled)

    def fetch(k):
        return cell_terms(load(0, k), load(1, k), load(2, k), load(3, k)) + (load(4, k),)

    def body(k, carry):
        now, flux_before, bed_before = carry
        after = fetch(jnp.minimum(k + 1, count - 1)) if count > 1 else now
        cell, bed = now[:8], now[8]
        up = tuple(upper(a, b) for a, b in zip(cell, after[:8]))
        y_flux = doubled_flux(swapped(cell), swapped(up))
        y_rolled = tuple(row_roll(f, 1) for f in y_flux)
        dy = tuple(f - lower(b, r) for f, b, r in zip(y_flux, flux_before, y_rolled))
        west = tuple(lane_roll(a, 1) for a in cell)
        x_flux = doubled_flux(west, cell)
        dx = tuple(lane_roll(f, -1) - f for f in x_flux)
        bed_rolled = row_roll(bed, 1)
        bed_y = upper(bed, after[8]) - lower(bed_before, bed_rolled)
        bed_x = lane_roll(bed, -1) - lane_roll(bed, 1)
        h, qx, qy, m = cell[:4]
        friction = load(5, k)
        step = 0.5 * TIME_STEP
        slope = (step * GRAVITY) * h
        new_h = h - step * (dx[0] + dy[0])
        new_x = qx - step * (dx[1] + dy[2]) - slope * bed_x
        new_y = qy - step * (dx[2] + dy[1]) - slope * bed_y
        new_m = m - step * (dx[3] + dy[3])
        inverse = new_h / (new_h * new_h + DRY_EPS)
        speed_x = new_x * inverse
        speed_y = new_y * inverse
        square = speed_x * speed_x + speed_y * speed_y
        speed = root_of(square)
        depth = jnp.maximum(new_h, 0.0) + 0.1
        factor = depth / (depth + TIME_STEP * friction * speed)
        conc = new_m * inverse
        net = EROSION * jnp.maximum(CAPACITY * square - conc, 0.0) - SETTLING * conc
        store(0, k, new_h)
        store(1, k, new_x * factor)
        store(2, k, new_y * factor)
        store(3, k, new_m + TIME_STEP * net)
        store(4, k, bed - (TIME_STEP / (1.0 - POROSITY)) * net)
        return after, y_rolled, bed_rolled

    zero = jnp.zeros((SUB, LANES), jnp.float32)
    start = (fetch(0), (zero,) * 4, zero)
    if count == 1:
        body(0, start)
    else:
        each = count // slices
        for part in range(slices):
            start = lax.fori_loop(part * each, (part + 1) * each, body, start, unroll=unroll)
            if pause is not None:
                pause(part)


def chunk(k):
    return pl.ds(pl.multiple_of(k * SUB, SUB), SUB)


def pack_frames(patches, frames, turned, slots):
    per_dev, _, extent, _ = patches.shape
    tiles = frames.shape[1]
    lanes = lane_index()

    def columns(k, _):
        total = jnp.zeros((SUB, LANES), jnp.float32)
        for p in range(per_dev):
            for f in range(tiles):
                value = patches[p, f, chunk(k), :]
                base = p * 32
                if f < 4:
                    spots = ((base + 2 * f, 2, 0), (base + 8 + 2 * f, 2, LANES - 2))
                elif f == 4:
                    spots = ((base + 16, 2, 0), (base + 18, 2, LANES - 2))
                else:
                    spots = ((base + 24, 1, 0), (base + 25, 1, LANES - 1))
                for spot, width, origin in spots:
                    inside = (lanes >= spot) & (lanes < spot + width)
                    total = jnp.where(inside, lane_roll(value, spot - origin), total)
        turned[chunk(k), :] = total
        return 0

    lax.fori_loop(0, extent // SUB, columns, 0, unroll=2)
    turned[...] = turned[...].T
    rows = row_index()
    low, high = slice(0, SUB), slice(extent - SUB, extent)
    for p in range(per_dev):
        base = p * 32
        out = frames.at[slots[p]]
        out[WEST] = turned[base : base + 8]
        out[EAST] = turned[base + 8 : base + 16]
        south = north = jnp.zeros((SUB, LANES), jnp.float32)
        for f in range(4):
            inside = (rows >= 2 * f) & (rows < 2 * f + 2)
            south = jnp.where(inside, row_roll(patches[p, f, low, :], 2 * f), south)
            north = jnp.where(inside, row_roll(patches[p, f, high, :], 2 * f + 2), north)
        out[SOUTH] = south
        out[NORTH] = north
        bed = turned[base + 16 : base + 24]
        bed = jnp.where((rows == 4) | (rows == 5), row_roll(patches[p, 4, low, :], 4), bed)
        bed = jnp.where(rows >= 6, patches[p, 4, high, :], bed)
        out[BED_TILE] = bed
        if tiles > FRICTION_TILE:
            rough = turned[base + 24 : base + 32]
            rough = jnp.where(rows == 2, row_roll(patches[p, 5, low, :], 2), rough)
            rough = jnp.where(rows == 3, row_roll(patches[p, 5, high, :], 4), rough)
            out[FRICTION_TILE] = rough


def kept_slots(migration, owner, per_dev):
    moves = migration.shape[1]
    rank = jnp.int32(0)
    slots = [jnp.int32(0)] * (per_dev - moves)
    for slot in range(per_dev):
        stays = jnp.int32(1)
        for k in range(moves):
            stays = stays * jnp.where(migration[owner, k] == slot, 0, 1)
        for j in range(per_dev - moves):
            slots[j] = jnp.where((stays == 1) & (rank == j), slot, slots[j])
        rank = rank + stays
    return slots + [migration[owner, k] for k in range(moves)]


def begin_kernel(device, migration, fields, mask, started, frames, turned):
    per_dev = fields.shape[0]
    slots = kept_slots(migration, device[0], per_dev)
    for p, slot in enumerate(slots):
        wet = mask[slot].astype(jnp.float32)
        for f in range(6):
            started[p, f] = fields[slot, f] * wet if f < 4 else fields[slot, f]
    pack_frames(started, frames, turned, slots)


def begin(device, migration, fields, mask):
    per_dev = fields.shape[0]
    return pl.pallas_call(
        begin_kernel,
        out_shape=(
            jax.ShapeDtypeStruct(fields.shape, jnp.float32),
            jax.ShapeDtypeStruct((per_dev, TILES, SUB, LANES), jnp.float32),
        ),
        in_specs=[SMEM, SMEM, VMEM, VMEM],
        out_specs=(VMEM, VMEM),
        scratch_shapes=[pltpu.VMEM((LANES, LANES), jnp.float32)],
        compiler_params=pltpu.CompilerParams(vmem_limit_bytes=VMEM_LIMIT),
    )(device, migration, fields, mask)


def gather_kernel(
    count, moves, patches, mine, pool, main, strip, edges,
    held, middle, own_sem, held_sem, move_send, move_recv, send_sem, recv_sem,
):
    per_dev, _, extent, _ = patches.shape
    chunks = extent // SUB
    length = count // 8
    me = lax.axis_index("curve")
    core, x, y, z = me % 2, (me // 2) % 2, (me // 4) % 2, me // 8
    other_core = me + 1 - 2 * core
    other_x = me + 2 - 4 * x
    other_y = me + 4 - 8 * y
    across = me + 6 - 4 * x - 8 * y
    has_up, has_down = z < length - 1, z > 0
    above = jnp.where(has_up, me + 8, me - 8)
    below = jnp.where(has_down, me - 8, me + 8)
    following = lax.rem(me + 1, count)
    previous = lax.rem(me + count - 1, count)

    local = []
    for p in range(per_dev - moves):
        local.append(pltpu.make_async_copy(patches.at[p], held.at[p], held_sem.at[p]))
        local[p].start()
    own_copy = pltpu.make_async_copy(mine, pool.at[pl.ds(me * per_dev, per_dev)], own_sem)
    own_copy.start()

    barrier = pltpu.get_barrier_semaphore()

    def greet(device):
        pl.semaphore_signal(
            barrier, inc=1, device_id=(device,), device_id_type=pl.DeviceIdType.MESH
        )

    friends = [other_core, other_x, other_y] + ([following, previous] if moves else [])
    for device in friends:
        greet(device)
    pl.when(has_up)(lambda: greet(above))
    pl.when(has_down)(lambda: greet(below))
    pl.semaphore_wait(
        barrier, len(friends) + has_up.astype(jnp.int32) + has_down.astype(jnp.int32)
    )

    def place(block):
        return pool.at[pl.ds(block * per_dev, per_dev)]

    def copy_of(block, device, slot, own):
        return pltpu.make_async_remote_copy(
            src_ref=mine if own else place(block),
            dst_ref=place(block),
            send_sem=send_sem.at[slot],
            recv_sem=recv_sem.at[block],
            device_id=(device,),
            device_id_type=pl.DeviceIdType.MESH,
        )

    def both(first, second):
        if first is None:
            return second
        return first if second is None else first & second

    def perform(when, action):
        if when is None:
            action()
        else:
            pl.when(when)(action)

    sends = []
    events = {}

    def send(at, block, device, when=None, own=False):
        slot = len(sends)
        sends.append((block, device, slot, own, when))

        def action():
            perform(when, lambda: copy_of(block, device, slot, own).start())

        events.setdefault(at, []).append(action)

    def arrive(at, block, when=None):
        def action():
            perform(when, lambda: copy_of(block, other_core, 0, False).wait_recv())

        events.setdefault(at, []).append(action)

    for device, when in (
        (above, has_up), (below, has_down), (other_x, None), (other_y, None), (other_core, None)
    ):
        send(-1, me, device, when, True)

    def sideways(at, level, when):
        x_block = level * 8 + other_x % 8
        y_block = level * 8 + other_y % 8
        arrive(at, x_block, when)
        send(at, x_block, other_y, both(level % 2 == 0, when))
        send(at, x_block, other_core, when)
        arrive(at, y_block, when)
        send(at, y_block, other_x, both(level % 2 == 1, when))
        send(at, y_block, other_core, when)

    levels = [[(z, None)]]
    for distance in range(1, length):
        levels.append(
            [(z - distance, z >= distance), (z + distance, z + distance < length)]
        )
    for distance in range(length):
        if distance:
            at = 3 * distance - 2
            for sign, (level, there) in zip((-1, 1), levels[distance]):
                block = level * 8 + me % 8
                arrive(at, block, there)
                if distance < length - 1:
                    if sign < 0:
                        send(at, block, above, there & has_up)
                    else:
                        send(at, block, below, there & has_down)
                send(at, block, other_x, there)
                send(at, block, other_y, there)
                send(at, block, other_core, there)
        for level in levels[distance]:
            sideways(3 * distance + 2, *level)
    for distance in range(length):
        at = 3 * length + 1 + distance
        for level, there in levels[distance]:
            block = level * 8 + across % 8
            arrive(at, block, there)
            send(at, block, other_core, there)

    def occur(at):
        for action in events.get(at, ()):
            action()

    occur(-1)
    moving = []
    for k in range(moves):
        moving.append(
            pltpu.make_async_remote_copy(
                src_ref=patches.at[per_dev - moves + k],
                dst_ref=held.at[per_dev - moves + k],
                send_sem=move_send.at[k],
                recv_sem=move_recv.at[k],
                device_id=(following,),
                device_id_type=pl.DeviceIdType.MESH,
            )
        )
        moving[k].start()

    slices = 2
    for copy in local:
        copy.wait()

    def main_patch(p, _):
        for k in range(moves):
            pl.when(p == per_dev - moves + k)(moving[k].wait_recv)
        start, end = held.at[p], main.at[p]
        for step, (source, target) in enumerate(((start, middle), (middle, end))):

            def load(f, k):
                return (start if f == 5 else source)[f, chunk(k), :]

            def store(f, k, value):
                target[f, chunk(k), :] = value

            def pause(part):
                for q in range(per_dev):
                    pl.when(p == q)(lambda: occur(q * 2 * slices + step * slices + part))

            advance_rows(load, store, chunks, 2, slices, pause)
        end[5] = start[5]
        return 0

    lax.fori_loop(0, per_dev, main_patch, 0)

    def fill_strip(k, _):
        for f in range(6):
            strip[f, chunk(k), :] = lay_strip([held[p, f, chunk(k), :] for p in range(per_dev)])
        return 0

    lax.fori_loop(0, chunks, fill_strip, 0, unroll=2)
    for p in range(per_dev):
        for f in range(6):
            edges[p, 0, f] = held[p, f, 0:SUB, :]
            edges[p, 1, f] = held[p, f, extent - SUB : extent, :]

    for at in sorted(events):
        if at >= 2 * slices * per_dev:
            occur(at)
    for column in range(4):
        for level in range(length):
            copy_of(level * 8 + 2 * column + other_core % 2, other_core, 0, False).wait_recv()
    own_copy.wait()
    for copy in moving:
        copy.wait_send()
    for block, device, slot, own, when in sends:
        perform(when, copy_of(block, device, slot, own).wait_send)


def lay_strip(values):
    lanes = lane_index()
    total = jnp.zeros((SUB, LANES), jnp.float32)
    for p, value in enumerate(values):
        for side, shift in ((WEST, 2), (EAST, 6)):
            group = 2 * p + side
            total = jnp.where(lanes // SUB == group, lane_roll(value, group * SUB + shift), total)
    return total


def gather_frames(patches, frames, count, moves, collective_id):
    per_dev, _, extent, _ = patches.shape

    def shape(*sizes):
        return jax.ShapeDtypeStruct(sizes, jnp.float32)

    return pl.pallas_call(
        functools.partial(gather_kernel, count, moves),
        out_shape=(
            shape(count * per_dev, *frames.shape[1:]),
            shape(*patches.shape),
            shape(6, extent, LANES),
            shape(per_dev, 2, 6, SUB, LANES),
        ),
        in_specs=[ANY, ANY],
        out_specs=(ANY, VMEM, VMEM, VMEM),
        scratch_shapes=[
            pltpu.VMEM(patches.shape, jnp.float32),
            pltpu.VMEM((6, extent, LANES), jnp.float32),
            pltpu.SemaphoreType.DMA,
            pltpu.SemaphoreType.DMA((per_dev,)),
            pltpu.SemaphoreType.DMA((max(moves, 1),)),
            pltpu.SemaphoreType.DMA((max(moves, 1),)),
            pltpu.SemaphoreType.DMA((5 * count,)),
            pltpu.SemaphoreType.DMA((count,)),
        ],
        compiler_params=pltpu.CompilerParams(
            collective_id=collective_id, has_side_effects=True, vmem_limit_bytes=VMEM_LIMIT
        ),
    )(patches, frames)


def step_kernel(count, second, device, neighbors, migration, main, own_strip, edges, pool, *refs):
    if second:
        rough_strip, rough_rows, ended, strip_a, strip_b, rows_a, rows_b, turned, halo = refs
    else:
        (ended, frames, rough_strip, rough_rows) = refs[:4]
        (strip_a, strip_b, rows_a, rows_b, turned, halo) = refs[4:]
    held_fields = 5 if second else 6
    per_dev, _, extent, _ = main.shape
    chunks = extent // SUB
    moves = migration.shape[1]
    owner = device[0]
    lanes, rows = lane_index(), row_index()

    def ring(value):
        return jnp.where(value < 0, value + count, jnp.where(value >= count, value - count, value))

    slots = kept_slots(migration, owner, per_dev)
    before = ring(owner - 1)
    held_patches = [owner * per_dev + slot for slot in slots[: per_dev - moves]]
    held_patches += [before * per_dev + migration[before, k] for k in range(moves)]

    def position(patch):
        if not second:
            return patch
        home = patch // per_dev
        slot = patch - home * per_dev
        result = patch
        for k in range(moves):
            result = result - jnp.where(migration[home, k] < slot, 1, 0)
        for k in range(moves):
            result = jnp.where(
                migration[home, k] == slot,
                ring(home + 1) * per_dev + per_dev - moves + k,
                result,
            )
        return result

    opposite = {WEST: EAST, EAST: WEST, SOUTH: NORTH, NORTH: SOUTH}

    def repaired(tile, side, missing):
        if side in (WEST, SOUTH):
            return jnp.where(everywhere(missing) & (rows % 2 == 1), row_roll(tile, 1), tile)
        return jnp.where(everywhere(missing) & (rows % 2 == 0), row_roll(tile, -1), tile)

    def bed_lines(source, side, missing):
        bed = pool[source, BED_TILE]
        bed = jnp.where(
            everywhere(missing), row_roll(bed, -2 * side), row_roll(bed, -2 * opposite[side])
        )
        return repaired(bed, side, missing)

    def by_field(patch, side, spot, near):
        beyond = neighbors[patch, side]
        missing = beyond < 0
        source = position(jnp.where(missing, patch, beyond))
        edge = jnp.where(missing, side, opposite[side])
        flow = repaired(pool[source, edge], side, missing)
        tiles = [row_roll(flow, spot - 2 * f) for f in range(4)]
        tiles.append(row_roll(bed_lines(source, side, missing), spot))
        if not second:
            rough = pool[source, FRICTION_TILE]
            tiles.append(
                jnp.where(
                    everywhere(missing),
                    row_roll(rough, near - side),
                    row_roll(rough, near - opposite[side]),
                )
            )
        return tiles

    for p in range(per_dev):
        patch = held_patches[p]
        for side, spot, near in ((WEST, 0, 1), (EAST, 6, 6)):
            group = 2 * p + side
            for f, tile in enumerate(by_field(patch, side, spot, near)):
                turned[f, group * SUB : (group + 1) * SUB] = tile
        for end, side, spot, near in ((0, SOUTH, 6, 7), (1, NORTH, 0, 0)):
            for f, tile in enumerate(by_field(patch, side, spot, near)):
                halo[p, end, f] = tile

    for f in range(held_fields):
        turned[f] = turned[f].T

    group_lane = lanes % SUB
    odd_group = (lanes // SUB) % 2
    from_halo = ((odd_group == 0) & (group_lane < 2)) | ((odd_group == 1) & (group_lane >= 6))

    def fill_strip(k, _):
        for f in range(held_fields):
            strip_a[f, chunk(k + 1), :] = jnp.where(
                from_halo, turned[f, chunk(k), :], own_strip[f, chunk(k), :]
            )
        return 0

    lax.fori_loop(0, chunks, fill_strip, 0, unroll=2)

    for end, side, row, line in ((0, SOUTH, 7, 1), (1, NORTH, 0, 0)):
        place = slice(0, SUB) if end == 0 else slice((chunks + 1) * SUB, (chunks + 2) * SUB)
        corner = [
            lay_strip([halo[p, end, f] for p in range(per_dev)]) for f in range(held_fields)
        ]
        for p in range(per_dev):
            patch = held_patches[p]
            beyond = neighbors[patch, side]
            missing = beyond < 0
            base = jnp.where(missing, patch, beyond)
            edge = jnp.where(missing, side, opposite[side])
            for across, spot, inner, outer in ((WEST, 1, 0, LANES - 1), (EAST, 6, LANES - 1, 0)):
                aside = neighbors[base, across]
                alone = everywhere(aside < 0)
                source = position(jnp.where(aside < 0, base, aside))
                lane = (2 * p + across) * SUB + spot
                flow = repaired(pool[source, edge], side, missing)
                bed = bed_lines(source, side, missing)
                flow = jnp.where(alone, lane_roll(flow, lane - inner), lane_roll(flow, lane - outer))
                bed = jnp.where(alone, lane_roll(bed, lane - inner), lane_roll(bed, lane - outer))
                here = (lanes == lane) & (rows == row)
                for f in range(4):
                    corner[f] = jnp.where(here, row_roll(flow, row - 2 * f - line), corner[f])
                corner[4] = jnp.where(here, row_roll(bed, row - line), corner[4])
        for f in range(held_fields):
            strip_a[f, place, :] = corner[f]

    for p in range(per_dev):
        for f in range(held_fields):
            rows_a[2 * p, f] = jnp.where(
                rows < 2, row_roll(halo[p, 0, f], 2), row_roll(edges[p, 0, f], 2)
            )
            rows_a[2 * p + 1, f] = jnp.where(
                rows >= 6, row_roll(halo[p, 1, f], 6), row_roll(edges[p, 1, f], -2)
            )

    if not second:
        rough_strip[...] = strip_a[5]
        for i in range(2 * per_dev):
            rough_rows[i] = rows_a[i, 5]

    def run(source, target):
        def load(f, k):
            return rough_strip[chunk(k), :] if f == 5 else source[f, chunk(k), :]

        def store(f, k, value):
            target[f, chunk(k), :] = value

        advance_rows(load, store, chunks + 2, 2)

    run(strip_a, strip_b)
    run(strip_b, strip_a)

    def row_strip(i, _):
        def step(source, target):
            def load(f, k):
                return rough_rows[i] if f == 5 else source[i, f]

            def store(f, k, value):
                target[i, f] = value

            advance_rows(load, store, 1, 1)

        step(rows_a, rows_b)
        step(rows_b, rows_a)
        return 0

    lax.fori_loop(0, 2 * per_dev, row_strip, 0, unroll=2)

    ends = slots if second else list(range(per_dev))

    def merge(k, _):
        for f in range(5):
            strip = strip_a[f, chunk(k + 1), :]
            for p in range(per_dev):
                value = main[p, f, chunk(k), :]
                value = jnp.where(
                    (rows < 2) & everywhere(k == 0), row_roll(rows_a[2 * p, f], -2), value
                )
                value = jnp.where(
                    (rows >= 6) & everywhere(k == chunks - 1),
                    row_roll(rows_a[2 * p + 1, f], 2),
                    value,
                )
                west = lane_roll(strip, -(2 * p * SUB + 2))
                east = lane_roll(strip, -6 - (2 * p + 1) * SUB)
                value = jnp.where(lanes < 2, west, value)
                ended[ends[p], f, chunk(k), :] = jnp.where(lanes >= LANES - 2, east, value)
        for p in range(per_dev):
            ended[ends[p], 5, chunk(k), :] = main[p, 5, chunk(k), :]
        return 0

    lax.fori_loop(0, chunks, merge, 0)
    if not second:
        pack_frames(ended, frames, turned.at[0], ends)


def finish_round(device, neighbors, migration, pieces, count, rough):
    pool, main, strip, edges = pieces
    second = rough is not None
    per_dev, _, extent, _ = main.shape

    def shape(*sizes):
        return jax.ShapeDtypeStruct(sizes, jnp.float32)

    rough_shapes = (shape(extent + 2 * SUB, LANES), shape(2 * per_dev, SUB, LANES))
    out_shape = (shape(*main.shape),)
    if not second:
        out_shape += (shape(per_dev, BED_TILE + 1, SUB, LANES),) + rough_shapes
    operands = (device, neighbors, migration, main, strip, edges, pool)
    if second:
        operands += rough
    return pl.pallas_call(
        functools.partial(step_kernel, count, second),
        out_shape=out_shape,
        in_specs=[SMEM] * 3 + [VMEM] * (len(operands) - 3),
        out_specs=(VMEM,) * len(out_shape),
        scratch_shapes=[
            pltpu.VMEM((6, extent + 2 * SUB, LANES), jnp.float32),
            pltpu.VMEM((6, extent + 2 * SUB, LANES), jnp.float32),
            pltpu.VMEM((2 * per_dev, 6, SUB, LANES), jnp.float32),
            pltpu.VMEM((2 * per_dev, 6, SUB, LANES), jnp.float32),
            pltpu.VMEM((6, LANES, LANES), jnp.float32),
            pltpu.VMEM((per_dev, 2, 6, SUB, LANES), jnp.float32),
        ],
        compiler_params=pltpu.CompilerParams(vmem_limit_bytes=VMEM_LIMIT),
    )(*operands)


def shards(fields, wet_mask, neighbors, migration):
    count = lax.axis_size("curve")
    moves = migration.shape[1]
    device = lax.axis_index("curve").astype(jnp.int32).reshape(1)
    started, frames = begin(device, migration, fields, wet_mask)
    pieces = gather_frames(started, frames, count, moves, 0)
    halfway, frames, *rough = finish_round(device, neighbors, migration, pieces, count, None)
    pieces = gather_frames(halfway, frames, count, 0, 1)
    (ended,) = finish_round(device, neighbors, migration, pieces, count, tuple(rough))
    return ended


def solution(mesh):
    placed = (P("curve", None, None, None), P("curve", None, None), P(), P())
    return jax.shard_map(
        shards, mesh=mesh, in_specs=placed, out_specs=P("curve", None, None, None), check_vma=False
    )
```

```python
import functools

import jax
import jax.numpy as jnp
from jax import lax
from jax.experimental import pallas as pl
from jax.experimental.pallas import tpu as pltpu
from jax.sharding import PartitionSpec as P

GRAVITY = 9.81
TIME_STEP = 0.04
DRY_EPS = 0.01
CAPACITY = 0.02
EROSION = 0.5
SETTLING = 0.2
POROSITY = 0.4

LANES = 128
SUB = 8
WEST, EAST, SOUTH, NORTH = range(4)
BED_TILE, FRICTION_TILE, TILES = 4, 5, 6
VMEM_LIMIT = 48 * 1024 * 1024
VMEM = pl.BlockSpec(memory_space=pltpu.VMEM)
SMEM = pl.BlockSpec(memory_space=pltpu.SMEM)
ANY = pl.BlockSpec(memory_space=pl.ANY)


def lane_index():
    return lax.broadcasted_iota(jnp.int32, (SUB, LANES), 1)


def row_index():
    return lax.broadcasted_iota(jnp.int32, (SUB, LANES), 0)


def lane_roll(value, shift):
    shift = shift % LANES
    return value if shift == 0 else pltpu.roll(value, shift, 1)


def row_roll(value, shift):
    shift = shift % SUB
    return value if shift == 0 else pltpu.roll(value, shift, 0)


def everywhere(flag):
    return jnp.full((SUB, LANES), flag.astype(jnp.int32)) > 0


def inverse_of(value):
    rough = pl.reciprocal(value, approx=True)
    return rough * (2.0 - value * rough)


def root_of(value):
    return value * lax.rsqrt(jnp.maximum(value, 1e-30))


def cell_terms(h, qx, qy, m):
    inverse = h * inverse_of(h * h + DRY_EPS)
    wet = jnp.maximum(h, 0.0)
    return (h, qx, qy, m, qx * inverse, qy * inverse, m * inverse, root_of(wet + 0.01))


def doubled_flux(left, right):
    h0, n0, t0, m0, u0, w0, s0, r0 = left
    h1, n1, t1, m1, u1, w1, s1, r1 = right
    scale = inverse_of(r0 + r1)
    part0 = r0 * scale
    part1 = r1 * scale
    mean_u = part0 * u0 + part1 * u1
    mean_w = part0 * w0 + part1 * w1
    mean_s = part0 * s0 + part1 * s1
    celerity = root_of((0.5 * GRAVITY) * (jnp.maximum(h0, 0.0) + jnp.maximum(h1, 0.0))) + 0.1
    half = 0.5 * inverse_of(celerity)
    dh = h1 - h0
    dn = n1 - n0
    plus = mean_u + celerity
    minus = mean_u - celerity
    p1 = jnp.abs(minus) * ((plus * dh - dn) * half)
    p3 = jnp.abs(plus) * ((dn - minus * dh) * half)
    both = p1 + p3
    middle = jnp.abs(mean_u)
    return (
        n0 + n1 - both,
        n0 * u0 + n1 * u1 + (0.5 * GRAVITY) * (h0 * h0 + h1 * h1) - (p1 * minus + p3 * plus),
        n0 * w0 + n1 * w1 - (both * mean_w + middle * (t1 - t0 - mean_w * dh)),
        n0 * s0 + n1 * s1 - (both * mean_s + middle * (m1 - m0 - mean_s * dh)),
    )


def swapped(cell):
    h, qx, qy, m, u, v, s, r = cell
    return (h, qy, qx, m, v, u, s, r)


def advance_rows(load, store, count, unroll, slices=1, pause=None):
    rows = row_index()
    first, last = rows == 0, rows == SUB - 1

    def upper(now, after):
        return row_roll(jnp.where(first, after, now), -1)

    def lower(before_rolled, rolled):
        return jnp.where(first, before_rolled, rolled)

    def fetch(k):
        return cell_terms(load(0, k), load(1, k), load(2, k), load(3, k)) + (load(4, k),)

    def body(k, carry):
        now, flux_before, bed_before = carry
        after = fetch(jnp.minimum(k + 1, count - 1)) if count > 1 else now
        cell, bed = now[:8], now[8]
        up = tuple(upper(a, b) for a, b in zip(cell, after[:8]))
        y_flux = doubled_flux(swapped(cell), swapped(up))
        y_rolled = tuple(row_roll(f, 1) for f in y_flux)
        dy = tuple(f - lower(b, r) for f, b, r in zip(y_flux, flux_before, y_rolled))
        west = tuple(lane_roll(a, 1) for a in cell)
        x_flux = doubled_flux(west, cell)
        dx = tuple(lane_roll(f, -1) - f for f in x_flux)
        bed_rolled = row_roll(bed, 1)
        bed_y = upper(bed, after[8]) - lower(bed_before, bed_rolled)
        bed_x = lane_roll(bed, -1) - lane_roll(bed, 1)
        h, qx, qy, m = cell[:4]
        friction = load(5, k)
        step = 0.5 * TIME_STEP
        slope = (step * GRAVITY) * h
        new_h = h - step * (dx[0] + dy[0])
        new_x = qx - step * (dx[1] + dy[2]) - slope * bed_x
        new_y = qy - step * (dx[2] + dy[1]) - slope * bed_y
        new_m = m - step * (dx[3] + dy[3])
        inverse = new_h * inverse_of(new_h * new_h + DRY_EPS)
        speed_x = new_x * inverse
        speed_y = new_y * inverse
        square = speed_x * speed_x + speed_y * speed_y
        speed = root_of(square)
        depth = jnp.maximum(new_h, 0.0) + 0.1
        factor = depth * inverse_of(depth + TIME_STEP * friction * speed)
        conc = new_m * inverse
        net = EROSION * jnp.maximum(CAPACITY * square - conc, 0.0) - SETTLING * conc
        store(0, k, new_h)
        store(1, k, new_x * factor)
        store(2, k, new_y * factor)
        store(3, k, new_m + TIME_STEP * net)
        store(4, k, bed - (TIME_STEP / (1.0 - POROSITY)) * net)
        return after, y_rolled, bed_rolled

    zero = jnp.zeros((SUB, LANES), jnp.float32)
    start = (fetch(0), (zero,) * 4, zero)
    if count == 1:
        body(0, start)
    else:
        each = count // slices
        for part in range(slices):
            start = lax.fori_loop(part * each, (part + 1) * each, body, start, unroll=unroll)
            if pause is not None:
                pause(part)


def chunk(k):
    return pl.ds(pl.multiple_of(k * SUB, SUB), SUB)


def pack_frames(patches, frames, turned, slots):
    per_dev, _, extent, _ = patches.shape
    tiles = frames.shape[1]
    lanes = lane_index()

    def columns(k, _):
        total = jnp.zeros((SUB, LANES), jnp.float32)
        for p in range(per_dev):
            for f in range(tiles):
                value = patches[p, f, chunk(k), :]
                base = p * 32
                if f < 4:
                    spots = ((base + 2 * f, 2, 0), (base + 8 + 2 * f, 2, LANES - 2))
                elif f == 4:
                    spots = ((base + 16, 2, 0), (base + 18, 2, LANES - 2))
                else:
                    spots = ((base + 24, 1, 0), (base + 25, 1, LANES - 1))
                for spot, width, origin in spots:
                    inside = (lanes >= spot) & (lanes < spot + width)
                    total = jnp.where(inside, lane_roll(value, spot - origin), total)
        turned[chunk(k), :] = total
        return 0

    lax.fori_loop(0, extent // SUB, columns, 0, unroll=2)
    turned[...] = turned[...].T
    rows = row_index()
    low, high = slice(0, SUB), slice(extent - SUB, extent)
    for p in range(per_dev):
        base = p * 32
        out = frames.at[slots[p]]
        out[WEST] = turned[base : base + 8]
        out[EAST] = turned[base + 8 : base + 16]
        south = north = jnp.zeros((SUB, LANES), jnp.float32)
        for f in range(4):
            inside = (rows >= 2 * f) & (rows < 2 * f + 2)
            south = jnp.where(inside, row_roll(patches[p, f, low, :], 2 * f), south)
            north = jnp.where(inside, row_roll(patches[p, f, high, :], 2 * f + 2), north)
        out[SOUTH] = south
        out[NORTH] = north
        bed = turned[base + 16 : base + 24]
        bed = jnp.where((rows == 4) | (rows == 5), row_roll(patches[p, 4, low, :], 4), bed)
        bed = jnp.where(rows >= 6, patches[p, 4, high, :], bed)
        out[BED_TILE] = bed
        if tiles > FRICTION_TILE:
            rough = turned[base + 24 : base + 32]
            rough = jnp.where(rows == 2, row_roll(patches[p, 5, low, :], 2), rough)
            rough = jnp.where(rows == 3, row_roll(patches[p, 5, high, :], 4), rough)
            out[FRICTION_TILE] = rough


def kept_slots(migration, owner, per_dev):
    moves = migration.shape[0]
    rank = jnp.int32(0)
    slots = [jnp.int32(0)] * (per_dev - moves)
    for slot in range(per_dev):
        stays = jnp.int32(1)
        for k in range(moves):
            stays = stays * jnp.where(migration[k, owner] == slot, 0, 1)
        for j in range(per_dev - moves):
            slots[j] = jnp.where((stays == 1) & (rank == j), slot, slots[j])
        rank = rank + stays
    return slots + [migration[k, owner] for k in range(moves)]


def begin_kernel(device, migration, fields, mask, started, frames, turned):
    per_dev = fields.shape[0]
    slots = kept_slots(migration, device[0], per_dev)
    for p, slot in enumerate(slots):
        wet = mask[slot].astype(jnp.float32)
        for f in range(6):
            started[p, f] = fields[slot, f] * wet if f < 4 else fields[slot, f]
    pack_frames(started, frames, turned, slots)


def begin(device, migration, fields, mask):
    per_dev = fields.shape[0]
    return pl.pallas_call(
        begin_kernel,
        out_shape=(
            jax.ShapeDtypeStruct(fields.shape, jnp.float32),
            jax.ShapeDtypeStruct((per_dev, TILES, SUB, LANES), jnp.float32),
        ),
        in_specs=[SMEM, SMEM, VMEM, VMEM],
        out_specs=(VMEM, VMEM),
        scratch_shapes=[pltpu.VMEM((LANES, LANES), jnp.float32)],
        compiler_params=pltpu.CompilerParams(vmem_limit_bytes=VMEM_LIMIT),
    )(device, migration, fields, mask)


def gather_kernel(
    count, moves, patches, mine, pool, main, strip, edges,
    held, middle, own_sem, held_sem, move_send, move_recv, send_sem, recv_sem,
):
    per_dev, _, extent, _ = patches.shape
    chunks = extent // SUB
    length = count // 8
    me = lax.axis_index("curve")
    core, x, y, z = me % 2, (me // 2) % 2, (me // 4) % 2, me // 8
    other_core = me + 1 - 2 * core
    other_x = me + 2 - 4 * x
    other_y = me + 4 - 8 * y
    across = me + 6 - 4 * x - 8 * y
    has_up, has_down = z < length - 1, z > 0
    above = jnp.where(has_up, me + 8, me - 8)
    below = jnp.where(has_down, me - 8, me + 8)
    following = lax.rem(me + 1, count)
    previous = lax.rem(me + count - 1, count)

    local = []
    for p in range(per_dev - moves):
        local.append(pltpu.make_async_copy(patches.at[p], held.at[p], held_sem.at[p]))
        local[p].start()
    own_copy = pltpu.make_async_copy(mine, pool.at[pl.ds(me * per_dev, per_dev)], own_sem)
    own_copy.start()

    barrier = pltpu.get_barrier_semaphore()

    def greet(device):
        pl.semaphore_signal(
            barrier, inc=1, device_id=(device,), device_id_type=pl.DeviceIdType.MESH
        )

    friends = [other_core, other_x, other_y] + ([following, previous] if moves else [])
    for device in friends:
        greet(device)
    pl.when(has_up)(lambda: greet(above))
    pl.when(has_down)(lambda: greet(below))
    pl.semaphore_wait(
        barrier, len(friends) + has_up.astype(jnp.int32) + has_down.astype(jnp.int32)
    )

    def place(block):
        return pool.at[pl.ds(block * per_dev, per_dev)]

    def copy_of(block, device, slot, own):
        return pltpu.make_async_remote_copy(
            src_ref=mine if own else place(block),
            dst_ref=place(block),
            send_sem=send_sem.at[slot],
            recv_sem=recv_sem.at[block],
            device_id=(device,),
            device_id_type=pl.DeviceIdType.MESH,
        )

    def both(first, second):
        if first is None:
            return second
        return first if second is None else first & second

    def perform(when, action):
        if when is None:
            action()
        else:
            pl.when(when)(action)

    sends = []
    events = {}

    def send(at, block, device, when=None, own=False):
        slot = len(sends)
        sends.append((block, device, slot, own, when))

        def action():
            perform(when, lambda: copy_of(block, device, slot, own).start())

        events.setdefault(at, []).append(action)

    def arrive(at, block, when=None):
        def action():
            perform(when, lambda: copy_of(block, other_core, 0, False).wait_recv())

        events.setdefault(at, []).append(action)

    for device, when in (
        (above, has_up), (below, has_down), (other_x, None), (other_y, None), (other_core, None)
    ):
        send(-1, me, device, when, True)

    def sideways(at, level, when):
        x_block = level * 8 + other_x % 8
        y_block = level * 8 + other_y % 8
        arrive(at, x_block, when)
        send(at, x_block, other_y, both(level % 2 == 0, when))
        send(at, x_block, other_core, when)
        arrive(at, y_block, when)
        send(at, y_block, other_x, both(level % 2 == 1, when))
        send(at, y_block, other_core, when)

    levels = [[(z, None)]]
    for distance in range(1, length):
        levels.append(
            [(z - distance, z >= distance), (z + distance, z + distance < length)]
        )
    for distance in range(length):
        if distance:
            at = 6 * distance - 1
            for sign, (level, there) in zip((-1, 1), levels[distance]):
                block = level * 8 + me % 8
                arrive(at, block, there)
                if distance < length - 1:
                    if sign < 0:
                        send(at, block, above, there & has_up)
                    else:
                        send(at, block, below, there & has_down)
                send(at, block, other_x, there)
                send(at, block, other_y, there)
                send(at, block, other_core, there)
        for level in levels[distance]:
            sideways(6 * distance + 6, *level)
    for distance in range(length):
        at = 6 * distance + 12
        for level, there in levels[distance]:
            block = level * 8 + across % 8
            arrive(at, block, there)
            send(at, block, other_core, there)

    def occur(at):
        for action in events.get(at, ()):
            action()

    occur(-1)
    moving = []
    for k in range(moves):
        moving.append(
            pltpu.make_async_remote_copy(
                src_ref=patches.at[per_dev - moves + k],
                dst_ref=held.at[per_dev - moves + k],
                send_sem=move_send.at[k],
                recv_sem=move_recv.at[k],
                device_id=(following,),
                device_id_type=pl.DeviceIdType.MESH,
            )
        )
        moving[k].start()

    slices = 4
    for copy in local:
        copy.wait()

    def main_patch(p, _):
        for k in range(moves):
            pl.when(p == per_dev - moves + k)(moving[k].wait_recv)
        start, end = held.at[p], main.at[p]
        for step, (source, target) in enumerate(((start, middle), (middle, end))):

            def load(f, k):
                return (start if f == 5 else source)[f, chunk(k), :]

            def store(f, k, value):
                target[f, chunk(k), :] = value

            def pause(part):
                for q in range(per_dev):
                    pl.when(p == q)(lambda: occur(q * 2 * slices + step * slices + part))

            advance_rows(load, store, chunks, 4, slices, pause)
        end[5] = start[5]
        return 0

    lax.fori_loop(0, per_dev, main_patch, 0)

    def fill_strip(k, _):
        for f in range(6):
            strip[f, chunk(k), :] = lay_strip([held[p, f, chunk(k), :] for p in range(per_dev)])
        return 0

    lax.fori_loop(0, chunks, fill_strip, 0, unroll=2)
    for p in range(per_dev):
        for f in range(6):
            edges[p, 0, f] = held[p, f, 0:SUB, :]
            edges[p, 1, f] = held[p, f, extent - SUB : extent, :]

    for at in sorted(events):
        if at >= 2 * slices * per_dev:
            occur(at)
    for column in range(4):
        for level in range(length):
            copy_of(level * 8 + 2 * column + other_core % 2, other_core, 0, False).wait_recv()
    own_copy.wait()
    for copy in moving:
        copy.wait_send()
    for block, device, slot, own, when in sends:
        perform(when, copy_of(block, device, slot, own).wait_send)


def lay_strip(values):
    lanes = lane_index()
    total = jnp.zeros((SUB, LANES), jnp.float32)
    for p, value in enumerate(values):
        for side, shift in ((WEST, 2), (EAST, 6)):
            group = 2 * p + side
            total = jnp.where(lanes // SUB == group, lane_roll(value, group * SUB + shift), total)
    return total


def gather_frames(patches, frames, count, moves, collective_id):
    per_dev, _, extent, _ = patches.shape

    def shape(*sizes):
        return jax.ShapeDtypeStruct(sizes, jnp.float32)

    return pl.pallas_call(
        functools.partial(gather_kernel, count, moves),
        out_shape=(
            shape(count * per_dev, *frames.shape[1:]),
            shape(*patches.shape),
            shape(6, extent, LANES),
            shape(per_dev, 2, 6, SUB, LANES),
        ),
        in_specs=[ANY, ANY],
        out_specs=(ANY, VMEM, VMEM, VMEM),
        scratch_shapes=[
            pltpu.VMEM(patches.shape, jnp.float32),
            pltpu.VMEM((6, extent, LANES), jnp.float32),
            pltpu.SemaphoreType.DMA,
            pltpu.SemaphoreType.DMA((per_dev,)),
            pltpu.SemaphoreType.DMA((max(moves, 1),)),
            pltpu.SemaphoreType.DMA((max(moves, 1),)),
            pltpu.SemaphoreType.DMA((5 * count,)),
            pltpu.SemaphoreType.DMA((count,)),
        ],
        compiler_params=pltpu.CompilerParams(
            collective_id=collective_id, has_side_effects=True, vmem_limit_bytes=VMEM_LIMIT
        ),
    )(patches, frames)


def step_kernel(count, second, device, neighbors, migration, main, own_strip, edges, pool, *refs):
    if second:
        rough_strip, rough_rows, ended, strip_a, strip_b, rows_a, rows_b, turned, halo = refs
    else:
        (ended, frames, rough_strip, rough_rows) = refs[:4]
        (strip_a, strip_b, rows_a, rows_b, turned, halo) = refs[4:]
    held_fields = 5 if second else 6
    per_dev, _, extent, _ = main.shape
    chunks = extent // SUB
    moves = migration.shape[0]
    owner = device[0]
    lanes, rows = lane_index(), row_index()

    def ring(value):
        return jnp.where(value < 0, value + count, jnp.where(value >= count, value - count, value))

    slots = kept_slots(migration, owner, per_dev)
    before = ring(owner - 1)
    held_patches = [owner * per_dev + slot for slot in slots[: per_dev - moves]]
    held_patches += [before * per_dev + migration[k, before] for k in range(moves)]

    def position(patch):
        if not second:
            return patch
        home = patch // per_dev
        slot = patch - home * per_dev
        result = patch
        for k in range(moves):
            result = result - jnp.where(migration[k, home] < slot, 1, 0)
        for k in range(moves):
            result = jnp.where(
                migration[k, home] == slot,
                ring(home + 1) * per_dev + per_dev - moves + k,
                result,
            )
        return result

    opposite = {WEST: EAST, EAST: WEST, SOUTH: NORTH, NORTH: SOUTH}

    def repaired(tile, side, missing):
        if side in (WEST, SOUTH):
            return jnp.where(everywhere(missing) & (rows % 2 == 1), row_roll(tile, 1), tile)
        return jnp.where(everywhere(missing) & (rows % 2 == 0), row_roll(tile, -1), tile)

    def bed_lines(source, side, missing):
        bed = pool[source, BED_TILE]
        bed = jnp.where(
            everywhere(missing), row_roll(bed, -2 * side), row_roll(bed, -2 * opposite[side])
        )
        return repaired(bed, side, missing)

    def by_field(patch, side, spot, near):
        beyond = neighbors[side, patch]
        missing = beyond < 0
        source = position(jnp.where(missing, patch, beyond))
        edge = jnp.where(missing, side, opposite[side])
        flow = repaired(pool[source, edge], side, missing)
        tiles = [row_roll(flow, spot - 2 * f) for f in range(4)]
        tiles.append(row_roll(bed_lines(source, side, missing), spot))
        if not second:
            rough = pool[source, FRICTION_TILE]
            tiles.append(
                jnp.where(
                    everywhere(missing),
                    row_roll(rough, near - side),
                    row_roll(rough, near - opposite[side]),
                )
            )
        return tiles

    for p in range(per_dev):
        patch = held_patches[p]
        for side, spot, near in ((WEST, 0, 1), (EAST, 6, 6)):
            group = 2 * p + side
            for f, tile in enumerate(by_field(patch, side, spot, near)):
                turned[f, group * SUB : (group + 1) * SUB] = tile
        for end, side, spot, near in ((0, SOUTH, 6, 7), (1, NORTH, 0, 0)):
            for f, tile in enumerate(by_field(patch, side, spot, near)):
                halo[p, end, f] = tile

    for f in range(held_fields):
        turned[f] = turned[f].T

    group_lane = lanes % SUB
    odd_group = (lanes // SUB) % 2
    from_halo = ((odd_group == 0) & (group_lane < 2)) | ((odd_group == 1) & (group_lane >= 6))

    def fill_strip(k, _):
        for f in range(held_fields):
            strip_a[f, chunk(k + 1), :] = jnp.where(
                from_halo, turned[f, chunk(k), :], own_strip[f, chunk(k), :]
            )
        return 0

    lax.fori_loop(0, chunks, fill_strip, 0, unroll=2)

    for end, side, row, line in ((0, SOUTH, 7, 1), (1, NORTH, 0, 0)):
        place = slice(0, SUB) if end == 0 else slice((chunks + 1) * SUB, (chunks + 2) * SUB)
        corner = [
            lay_strip([halo[p, end, f] for p in range(per_dev)]) for f in range(held_fields)
        ]
        for p in range(per_dev):
            patch = held_patches[p]
            beyond = neighbors[side, patch]
            missing = beyond < 0
            base = jnp.where(missing, patch, beyond)
            edge = jnp.where(missing, side, opposite[side])
            for across, spot, inner, outer in ((WEST, 1, 0, LANES - 1), (EAST, 6, LANES - 1, 0)):
                aside = neighbors[across, base]
                alone = everywhere(aside < 0)
                source = position(jnp.where(aside < 0, base, aside))
                lane = (2 * p + across) * SUB + spot
                flow = repaired(pool[source, edge], side, missing)
                bed = bed_lines(source, side, missing)
                flow = jnp.where(alone, lane_roll(flow, lane - inner), lane_roll(flow, lane - outer))
                bed = jnp.where(alone, lane_roll(bed, lane - inner), lane_roll(bed, lane - outer))
                here = (lanes == lane) & (rows == row)
                for f in range(4):
                    corner[f] = jnp.where(here, row_roll(flow, row - 2 * f - line), corner[f])
                corner[4] = jnp.where(here, row_roll(bed, row - line), corner[4])
        for f in range(held_fields):
            strip_a[f, place, :] = corner[f]

    for p in range(per_dev):
        for f in range(held_fields):
            rows_a[2 * p, f] = jnp.where(
                rows < 2, row_roll(halo[p, 0, f], 2), row_roll(edges[p, 0, f], 2)
            )
            rows_a[2 * p + 1, f] = jnp.where(
                rows >= 6, row_roll(halo[p, 1, f], 6), row_roll(edges[p, 1, f], -2)
            )

    if not second:
        rough_strip[...] = strip_a[5]
        for i in range(2 * per_dev):
            rough_rows[i] = rows_a[i, 5]

    def run(source, target):
        def load(f, k):
            return rough_strip[chunk(k), :] if f == 5 else source[f, chunk(k), :]

        def store(f, k, value):
            target[f, chunk(k), :] = value

        advance_rows(load, store, chunks + 2, 2)

    run(strip_a, strip_b)
    run(strip_b, strip_a)

    def row_strip(i, _):
        def step(source, target):
            def load(f, k):
                return rough_rows[i] if f == 5 else source[i, f]

            def store(f, k, value):
                target[i, f] = value

            advance_rows(load, store, 1, 1)

        step(rows_a, rows_b)
        step(rows_b, rows_a)
        return 0

    lax.fori_loop(0, 2 * per_dev, row_strip, 0, unroll=2)

    ends = slots if second else list(range(per_dev))

    def merge(k, _):
        for f in range(5):
            strip = strip_a[f, chunk(k + 1), :]
            for p in range(per_dev):
                value = main[p, f, chunk(k), :]
                value = jnp.where(
                    (rows < 2) & everywhere(k == 0), row_roll(rows_a[2 * p, f], -2), value
                )
                value = jnp.where(
                    (rows >= 6) & everywhere(k == chunks - 1),
                    row_roll(rows_a[2 * p + 1, f], 2),
                    value,
                )
                west = lane_roll(strip, -(2 * p * SUB + 2))
                east = lane_roll(strip, -6 - (2 * p + 1) * SUB)
                value = jnp.where(lanes < 2, west, value)
                ended[ends[p], f, chunk(k), :] = jnp.where(lanes >= LANES - 2, east, value)
        for p in range(per_dev):
            ended[ends[p], 5, chunk(k), :] = main[p, 5, chunk(k), :]
        return 0

    lax.fori_loop(0, chunks, merge, 0)
    if not second:
        pack_frames(ended, frames, turned.at[0], ends)


def finish_round(device, neighbors, migration, pieces, count, rough):
    pool, main, strip, edges = pieces
    second = rough is not None
    per_dev, _, extent, _ = main.shape

    def shape(*sizes):
        return jax.ShapeDtypeStruct(sizes, jnp.float32)

    rough_shapes = (shape(extent + 2 * SUB, LANES), shape(2 * per_dev, SUB, LANES))
    out_shape = (shape(*main.shape),)
    if not second:
        out_shape += (shape(per_dev, BED_TILE + 1, SUB, LANES),) + rough_shapes
    operands = (device, neighbors, migration, main, strip, edges, pool)
    if second:
        operands += rough
    return pl.pallas_call(
        functools.partial(step_kernel, count, second),
        out_shape=out_shape,
        in_specs=[SMEM] * 3 + [VMEM] * (len(operands) - 3),
        out_specs=(VMEM,) * len(out_shape),
        scratch_shapes=[
            pltpu.VMEM((6, extent + 2 * SUB, LANES), jnp.float32),
            pltpu.VMEM((6, extent + 2 * SUB, LANES), jnp.float32),
            pltpu.VMEM((2 * per_dev, 6, SUB, LANES), jnp.float32),
            pltpu.VMEM((2 * per_dev, 6, SUB, LANES), jnp.float32),
            pltpu.VMEM((6, LANES, LANES), jnp.float32),
            pltpu.VMEM((per_dev, 2, 6, SUB, LANES), jnp.float32),
        ],
        compiler_params=pltpu.CompilerParams(vmem_limit_bytes=VMEM_LIMIT),
    )(*operands)


def shards(fields, wet_mask, neighbors, migration):
    count = lax.axis_size("curve")
    moves = migration.shape[1]
    device = lax.axis_index("curve").astype(jnp.int32).reshape(1)
    neighbors, migration = neighbors.T, migration.T
    started, frames = begin(device, migration, fields, wet_mask)
    pieces = gather_frames(started, frames, count, moves, 0)
    halfway, frames, *rough = finish_round(device, neighbors, migration, pieces, count, None)
    pieces = gather_frames(halfway, frames, count, 0, 1)
    (ended,) = finish_round(device, neighbors, migration, pieces, count, tuple(rough))
    return ended


def solution(mesh):
    placed = (P("curve", None, None, None), P("curve", None, None), P(), P())
    return jax.shard_map(
        shards, mesh=mesh, in_specs=placed, out_specs=P("curve", None, None, None), check_vma=False
    )
```

```python
import functools

import jax
import jax.numpy as jnp
from jax import lax
from jax.experimental import pallas as pl
from jax.experimental.pallas import tpu as pltpu
from jax.sharding import PartitionSpec as P

GRAVITY = 9.81
TIME_STEP = 0.04
DRY_EPS = 0.01
CAPACITY = 0.02
EROSION = 0.5
SETTLING = 0.2
POROSITY = 0.4

LANES = 128
SUB = 8
WEST, EAST, SOUTH, NORTH = range(4)
BED_TILE, PATCH_TILES = 4, 5
VMEM_LIMIT = 48 * 1024 * 1024
VMEM = pl.BlockSpec(memory_space=pltpu.VMEM)
SMEM = pl.BlockSpec(memory_space=pltpu.SMEM)
ANY = pl.BlockSpec(memory_space=pl.ANY)


def lane_index():
    return lax.broadcasted_iota(jnp.int32, (SUB, LANES), 1)


def row_index():
    return lax.broadcasted_iota(jnp.int32, (SUB, LANES), 0)


def lane_roll(value, shift):
    shift = shift % LANES
    return value if shift == 0 else pltpu.roll(value, shift, 1)


def row_roll(value, shift):
    shift = shift % SUB
    return value if shift == 0 else pltpu.roll(value, shift, 0)


def everywhere(flag):
    return jnp.full((SUB, LANES), flag.astype(jnp.int32)) > 0


def inverse_of(value):
    rough = pl.reciprocal(value, approx=True)
    return rough * (2.0 - value * rough)


def root_of(value):
    return value * lax.rsqrt(jnp.maximum(value, 1e-30))


def cell_terms(h, qx, qy, m):
    inverse = h * inverse_of(h * h + DRY_EPS)
    wet = jnp.maximum(h, 0.0)
    return (h, qx, qy, m, qx * inverse, qy * inverse, m * inverse, root_of(wet + 0.01))


def doubled_flux(left, right):
    h0, n0, t0, m0, u0, w0, s0, r0 = left
    h1, n1, t1, m1, u1, w1, s1, r1 = right
    scale = inverse_of(r0 + r1)
    part0 = r0 * scale
    part1 = r1 * scale
    mean_u = part0 * u0 + part1 * u1
    mean_w = part0 * w0 + part1 * w1
    mean_s = part0 * s0 + part1 * s1
    celerity = root_of((0.5 * GRAVITY) * (jnp.maximum(h0, 0.0) + jnp.maximum(h1, 0.0))) + 0.1
    half = 0.5 * inverse_of(celerity)
    dh = h1 - h0
    dn = n1 - n0
    plus = mean_u + celerity
    minus = mean_u - celerity
    p1 = jnp.abs(minus) * ((plus * dh - dn) * half)
    p3 = jnp.abs(plus) * ((dn - minus * dh) * half)
    both = p1 + p3
    middle = jnp.abs(mean_u)
    return (
        n0 + n1 - both,
        n0 * u0 + n1 * u1 + (0.5 * GRAVITY) * (h0 * h0 + h1 * h1) - (p1 * minus + p3 * plus),
        n0 * w0 + n1 * w1 - (both * mean_w + middle * (t1 - t0 - mean_w * dh)),
        n0 * s0 + n1 * s1 - (both * mean_s + middle * (m1 - m0 - mean_s * dh)),
    )


def swapped(cell):
    h, qx, qy, m, u, v, s, r = cell
    return (h, qy, qx, m, v, u, s, r)


def advance_rows(load, store, count, unroll, slices=1, pause=None):
    rows = row_index()
    first, last = rows == 0, rows == SUB - 1

    def upper(now, after):
        return row_roll(jnp.where(first, after, now), -1)

    def lower(before_rolled, rolled):
        return jnp.where(first, before_rolled, rolled)

    def fetch(k):
        return cell_terms(load(0, k), load(1, k), load(2, k), load(3, k)) + (load(4, k),)

    def body(k, carry):
        now, flux_before, bed_before = carry
        after = fetch(jnp.minimum(k + 1, count - 1)) if count > 1 else now
        cell, bed = now[:8], now[8]
        up = tuple(upper(a, b) for a, b in zip(cell, after[:8]))
        y_flux = doubled_flux(swapped(cell), swapped(up))
        y_rolled = tuple(row_roll(f, 1) for f in y_flux)
        dy = tuple(f - lower(b, r) for f, b, r in zip(y_flux, flux_before, y_rolled))
        west = tuple(lane_roll(a, 1) for a in cell)
        x_flux = doubled_flux(west, cell)
        dx = tuple(lane_roll(f, -1) - f for f in x_flux)
        bed_rolled = row_roll(bed, 1)
        bed_y = upper(bed, after[8]) - lower(bed_before, bed_rolled)
        bed_x = lane_roll(bed, -1) - lane_roll(bed, 1)
        h, qx, qy, m = cell[:4]
        friction = load(5, k)
        step = 0.5 * TIME_STEP
        slope = (step * GRAVITY) * h
        new_h = h - step * (dx[0] + dy[0])
        new_x = qx - step * (dx[1] + dy[2]) - slope * bed_x
        new_y = qy - step * (dx[2] + dy[1]) - slope * bed_y
        new_m = m - step * (dx[3] + dy[3])
        inverse = new_h * inverse_of(new_h * new_h + DRY_EPS)
        speed_x = new_x * inverse
        speed_y = new_y * inverse
        square = speed_x * speed_x + speed_y * speed_y
        speed = root_of(square)
        depth = jnp.maximum(new_h, 0.0) + 0.1
        factor = depth * inverse_of(depth + TIME_STEP * friction * speed)
        conc = new_m * inverse
        net = EROSION * jnp.maximum(CAPACITY * square - conc, 0.0) - SETTLING * conc
        store(0, k, new_h)
        store(1, k, new_x * factor)
        store(2, k, new_y * factor)
        store(3, k, new_m + TIME_STEP * net)
        store(4, k, bed - (TIME_STEP / (1.0 - POROSITY)) * net)
        return after, y_rolled, bed_rolled

    zero = jnp.zeros((SUB, LANES), jnp.float32)
    start = (fetch(0), (zero,) * 4, zero)
    if count == 1:
        body(0, start)
    else:
        each = count // slices
        for part in range(slices):
            start = lax.fori_loop(part * each, (part + 1) * each, body, start, unroll=unroll)
            if pause is not None:
                pause(part)


def chunk(k):
    return pl.ds(pl.multiple_of(k * SUB, SUB), SUB)


def pack_frames(patches, frames, turned, with_friction):
    per_dev, _, extent, _ = patches.shape
    fields = 6 if with_friction else 5
    lanes = lane_index()

    def columns(k, _):
        total = jnp.zeros((SUB, LANES), jnp.float32)
        for p in range(per_dev):
            for f in range(fields):
                value = patches[p, f, chunk(k), :]
                base = p * 32
                if f < 4:
                    spots = ((base + 2 * f, 2, 0), (base + 8 + 2 * f, 2, LANES - 2))
                elif f == 4:
                    spots = ((base + 16, 2, 0), (base + 18, 2, LANES - 2))
                else:
                    spots = ((base + 24, 1, 0), (base + 25, 1, LANES - 1))
                for spot, width, origin in spots:
                    inside = (lanes >= spot) & (lanes < spot + width)
                    total = jnp.where(inside, lane_roll(value, spot - origin), total)
        turned[chunk(k), :] = total
        return 0

    lax.fori_loop(0, extent // SUB, columns, 0, unroll=2)
    turned[...] = turned[...].T
    rows = row_index()
    low, high = slice(0, SUB), slice(extent - SUB, extent)
    for p in range(per_dev):
        base = p * 32
        out = frames.at[pl.ds(p * PATCH_TILES, PATCH_TILES)]
        out[WEST] = turned[base : base + 8]
        out[EAST] = turned[base + 8 : base + 16]
        south = north = jnp.zeros((SUB, LANES), jnp.float32)
        for f in range(4):
            inside = (rows >= 2 * f) & (rows < 2 * f + 2)
            south = jnp.where(inside, row_roll(patches[p, f, low, :], 2 * f), south)
            north = jnp.where(inside, row_roll(patches[p, f, high, :], 2 * f + 2), north)
        out[SOUTH] = south
        out[NORTH] = north
        bed = turned[base + 16 : base + 24]
        bed = jnp.where((rows == 4) | (rows == 5), row_roll(patches[p, 4, low, :], 4), bed)
        bed = jnp.where(rows >= 6, patches[p, 4, high, :], bed)
        out[BED_TILE] = bed
        if with_friction:
            rough = turned[base + 24 : base + 32]
            rough = jnp.where(rows == 2, row_roll(patches[p, 5, low, :], 2), rough)
            rough = jnp.where(rows == 3, row_roll(patches[p, 5, high, :], 4), rough)
            if p % 2 == 0:
                paired = rough
            else:
                paired = jnp.where(rows < 4, paired, row_roll(rough, 4))
            if p % 2 == 1 or p == per_dev - 1:
                frames[per_dev * PATCH_TILES + p // 2] = paired


def kept_slots(migration, owner, per_dev):
    moves = migration.shape[0]
    rank = jnp.int32(0)
    slots = [jnp.int32(0)] * (per_dev - moves)
    for slot in range(per_dev):
        stays = jnp.int32(1)
        for k in range(moves):
            stays = stays * jnp.where(migration[k, owner] == slot, 0, 1)
        for j in range(per_dev - moves):
            slots[j] = jnp.where((stays == 1) & (rank == j), slot, slots[j])
        rank = rank + stays
    return slots + [migration[k, owner] for k in range(moves)]


def begin_kernel(device, migration, fields, mask, started, frames, turned):
    per_dev = fields.shape[0]
    slots = kept_slots(migration, device[0], per_dev)
    for p, slot in enumerate(slots):
        wet = mask[slot].astype(jnp.float32)
        for f in range(6):
            started[p, f] = fields[slot, f] * wet if f < 4 else fields[slot, f]
    pack_frames(started, frames, turned, True)


def begin(device, migration, fields, mask):
    per_dev = fields.shape[0]
    return pl.pallas_call(
        begin_kernel,
        out_shape=(
            jax.ShapeDtypeStruct(fields.shape, jnp.float32),
            jax.ShapeDtypeStruct(
                (per_dev * PATCH_TILES + (per_dev + 1) // 2, SUB, LANES), jnp.float32
            ),
        ),
        in_specs=[SMEM, SMEM, VMEM, VMEM],
        out_specs=(VMEM, VMEM),
        scratch_shapes=[pltpu.VMEM((LANES, LANES), jnp.float32)],
        compiler_params=pltpu.CompilerParams(vmem_limit_bytes=VMEM_LIMIT),
    )(device, migration, fields, mask)


def gather_kernel(
    count, moves, patches, mine, pool, main, strip, edges,
    held, middle, own_sem, held_sem, move_send, move_recv, send_sem, recv_sem,
):
    per_dev, _, extent, _ = patches.shape
    chunks = extent // SUB
    length = count // 8
    me = lax.axis_index("curve")
    core, x, y, z = me % 2, (me // 2) % 2, (me // 4) % 2, me // 8
    other_core = me + 1 - 2 * core
    other_x = me + 2 - 4 * x
    other_y = me + 4 - 8 * y
    across = me + 6 - 4 * x - 8 * y
    has_up, has_down = z < length - 1, z > 0
    above = jnp.where(has_up, me + 8, me - 8)
    below = jnp.where(has_down, me - 8, me + 8)
    following = lax.rem(me + 1, count)
    previous = lax.rem(me + count - 1, count)

    local = []
    for p in range(per_dev - moves):
        local.append(pltpu.make_async_copy(patches.at[p], held.at[p], held_sem.at[p]))
        local[p].start()
    tiles = mine.shape[0]
    first_tiles = tiles - tiles // 4
    parts = ((0, first_tiles), (first_tiles, tiles - first_tiles))
    own_copy = pltpu.make_async_copy(mine, pool.at[pl.ds(me * tiles, tiles)], own_sem)
    own_copy.start()

    barrier = pltpu.get_barrier_semaphore()

    def greet(device):
        pl.semaphore_signal(
            barrier, inc=1, device_id=(device,), device_id_type=pl.DeviceIdType.MESH
        )

    friends = [other_core, other_x, other_y] + ([following, previous] if moves else [])
    for device in friends:
        greet(device)
    pl.when(has_up)(lambda: greet(above))
    pl.when(has_down)(lambda: greet(below))
    pl.semaphore_wait(
        barrier, len(friends) + has_up.astype(jnp.int32) + has_down.astype(jnp.int32)
    )

    def copy_of(block, device, slot, own, part):
        start, size = parts[part]
        target = pool.at[pl.ds(block * tiles + start, size)]
        return pltpu.make_async_remote_copy(
            src_ref=mine.at[pl.ds(start, size)] if own else target,
            dst_ref=target,
            send_sem=send_sem.at[slot],
            recv_sem=recv_sem.at[block * 2 + part],
            device_id=(device,),
            device_id_type=pl.DeviceIdType.MESH,
        )

    def both(first, second):
        if first is None:
            return second
        return first if second is None else first & second

    def perform(when, action):
        if when is None:
            action()
        else:
            pl.when(when)(action)

    sends = []
    events = {}

    def send(at, part, block, device, when=None, own=False):
        slot = len(sends)
        sends.append((block, device, slot, own, part, when))

        def action():
            perform(when, lambda: copy_of(block, device, slot, own, part).start())

        events.setdefault(at, []).append(action)

    def arrive(at, part, block, when=None):
        def action():
            perform(when, lambda: copy_of(block, other_core, 0, False, part).wait_recv())

        events.setdefault(at, []).append(action)

    for part in (1, 0):
        for device, when in (
            (above, has_up), (below, has_down), (other_x, None), (other_y, None), (other_core, None)
        ):
            send(-1, part, me, device, when, True)

    levels = [[(z, None)]]
    for distance in range(1, length):
        levels.append(
            [(z - distance, z >= distance), (z + distance, z + distance < length)]
        )

    def beside(at, part, level, when, onward):
        x_block = level * 8 + other_x % 8
        y_block = level * 8 + other_y % 8
        for block, turn, device in (
            (x_block, level % 2 == 0, other_y), (y_block, level % 2 == 1, other_x)
        ):
            arrive(at, part, block, when)
            send(at, part, block, device, both(turn, when))
            for further, there in onward:
                send(at, part, block, further, both(there, when))

    def along(at, part, distance, sign, column, there, onward):
        level = z + sign * distance
        block = level * 8 + column
        arrive(at, part, block, there)
        if distance < length - 1:
            if sign < 0:
                send(at, part, block, above, there & has_up)
            else:
                send(at, part, block, below, there & has_down)
        for device in onward:
            send(at, part, block, device, there)

    for distance in range(length):
        if distance:
            for sign, (_, there) in zip((-1, 1), levels[distance]):
                along(
                    5 * distance - 1, 0, distance, sign, me % 8, there,
                    (other_x, other_y, other_core),
                )
        for level, there in levels[distance]:
            beside(5 * distance + 5, 0, level, there, ((other_core, None),))
            block = level * 8 + across % 8
            arrive(5 * distance + 10, 0, block, there)
            send(5 * distance + 10, 0, block, other_core, there)
    vertical = ((above, has_up), (below, has_down), (other_core, None))
    beside(3, 1, z, None, vertical)
    arrive(5, 1, across)
    for device, there in vertical:
        send(5, 1, across, device, there)
    for distance in range(1, length):
        for sign, (_, there) in zip((-1, 1), levels[distance]):
            for column in (me % 8, other_x % 8, other_y % 8, across % 8):
                along(6 * distance + 2, 1, distance, sign, column, there, (other_core,))

    def occur(at):
        for action in events.get(at, ()):
            action()

    occur(-1)
    moving = []
    for k in range(moves):
        moving.append(
            pltpu.make_async_remote_copy(
                src_ref=patches.at[per_dev - moves + k],
                dst_ref=held.at[per_dev - moves + k],
                send_sem=move_send.at[k],
                recv_sem=move_recv.at[k],
                device_id=(following,),
                device_id_type=pl.DeviceIdType.MESH,
            )
        )
        moving[k].start()

    slices = 4
    for copy in local:
        copy.wait()

    def main_patch(p, _):
        for k in range(moves):
            pl.when(p == per_dev - moves + k)(moving[k].wait_recv)
        start, end = held.at[p], main.at[p]
        for step, (source, target) in enumerate(((start, middle), (middle, end))):

            def load(f, k):
                return (start if f == 5 else source)[f, chunk(k), :]

            def store(f, k, value):
                target[f, chunk(k), :] = value

            def pause(part):
                for q in range(per_dev):
                    pl.when(p == q)(lambda: occur(q * 2 * slices + step * slices + part))

            advance_rows(load, store, chunks, 4, slices, pause)
        end[5] = start[5]
        return 0

    lax.fori_loop(0, per_dev, main_patch, 0)

    def fill_strip(k, _):
        for f in range(6):
            strip[f, chunk(k), :] = lay_strip([held[p, f, chunk(k), :] for p in range(per_dev)])
        return 0

    lax.fori_loop(0, chunks, fill_strip, 0, unroll=2)
    for p in range(per_dev):
        for f in range(6):
            edges[p, 0, f] = held[p, f, 0:SUB, :]
            edges[p, 1, f] = held[p, f, extent - SUB : extent, :]

    for at in sorted(events):
        if at >= 2 * slices * per_dev:
            occur(at)
    for column in range(4):
        for level in range(length):
            for part in range(2):
                block = level * 8 + 2 * column + other_core % 2
                copy_of(block, other_core, 0, False, part).wait_recv()
    own_copy.wait()
    for copy in moving:
        copy.wait_send()
    for block, device, slot, own, part, when in sends:
        perform(when, copy_of(block, device, slot, own, part).wait_send)


def lay_strip(values):
    lanes = lane_index()
    total = jnp.zeros((SUB, LANES), jnp.float32)
    for p, value in enumerate(values):
        for side, shift in ((WEST, 2), (EAST, 6)):
            group = 2 * p + side
            total = jnp.where(lanes // SUB == group, lane_roll(value, group * SUB + shift), total)
    return total


def gather_frames(patches, frames, count, moves, collective_id):
    per_dev, _, extent, _ = patches.shape

    def shape(*sizes):
        return jax.ShapeDtypeStruct(sizes, jnp.float32)

    return pl.pallas_call(
        functools.partial(gather_kernel, count, moves),
        out_shape=(
            shape(count * frames.shape[0], *frames.shape[1:]),
            shape(*patches.shape),
            shape(6, extent, LANES),
            shape(per_dev, 2, 6, SUB, LANES),
        ),
        in_specs=[ANY, ANY],
        out_specs=(ANY, VMEM, VMEM, VMEM),
        scratch_shapes=[
            pltpu.VMEM(patches.shape, jnp.float32),
            pltpu.VMEM((6, extent, LANES), jnp.float32),
            pltpu.SemaphoreType.DMA,
            pltpu.SemaphoreType.DMA((per_dev,)),
            pltpu.SemaphoreType.DMA((max(moves, 1),)),
            pltpu.SemaphoreType.DMA((max(moves, 1),)),
            pltpu.SemaphoreType.DMA((8 * count,)),
            pltpu.SemaphoreType.DMA((2 * count,)),
        ],
        compiler_params=pltpu.CompilerParams(
            collective_id=collective_id, has_side_effects=True, vmem_limit_bytes=VMEM_LIMIT
        ),
    )(patches, frames)


def step_kernel(count, second, device, neighbors, migration, main, own_strip, edges, pool, *refs):
    if second:
        rough_strip, rough_rows, ended, strip_a, strip_b, rows_a, rows_b, turned, halo = refs
    else:
        (ended, frames, rough_strip, rough_rows) = refs[:4]
        (strip_a, strip_b, rows_a, rows_b, turned, halo) = refs[4:]
    held_fields = 5 if second else 6
    per_dev, _, extent, _ = main.shape
    chunks = extent // SUB
    moves = migration.shape[0]
    owner = device[0]
    lanes, rows = lane_index(), row_index()

    def ring(value):
        return jnp.where(value < 0, value + count, jnp.where(value >= count, value - count, value))

    slots = kept_slots(migration, owner, per_dev)
    before = ring(owner - 1)
    held_patches = [owner * per_dev + slot for slot in slots[: per_dev - moves]]
    held_patches += [before * per_dev + migration[k, before] for k in range(moves)]

    tiles = pool.shape[0] // count

    def spot_of(patch):
        home = patch // per_dev
        slot = patch - home * per_dev
        block, place = home, slot
        for k in range(moves):
            place = place - jnp.where(migration[k, home] < slot, 1, 0)
        for k in range(moves):
            here = migration[k, home] == slot
            place = jnp.where(here, per_dev - moves + k, place)
            if second:
                block = jnp.where(here, ring(home + 1), block)
        return block, place

    def tile_of(spot, tile):
        return pool[spot[0] * tiles + spot[1] * PATCH_TILES + tile]

    def friction_of(spot):
        tile = pool[spot[0] * tiles + per_dev * PATCH_TILES + spot[1] // 2]
        return jnp.where(everywhere(spot[1] % 2 == 1), row_roll(tile, 4), tile)

    opposite = {WEST: EAST, EAST: WEST, SOUTH: NORTH, NORTH: SOUTH}

    def repaired(tile, side, missing):
        if side in (WEST, SOUTH):
            return jnp.where(everywhere(missing) & (rows % 2 == 1), row_roll(tile, 1), tile)
        return jnp.where(everywhere(missing) & (rows % 2 == 0), row_roll(tile, -1), tile)

    def bed_lines(source, side, missing):
        bed = tile_of(source, BED_TILE)
        bed = jnp.where(
            everywhere(missing), row_roll(bed, -2 * side), row_roll(bed, -2 * opposite[side])
        )
        return repaired(bed, side, missing)

    def by_field(patch, side, spot, near):
        beyond = neighbors[side, patch]
        missing = beyond < 0
        source = spot_of(jnp.where(missing, patch, beyond))
        edge = jnp.where(missing, side, opposite[side])
        flow = repaired(tile_of(source, edge), side, missing)
        tiles = [row_roll(flow, spot - 2 * f) for f in range(4)]
        tiles.append(row_roll(bed_lines(source, side, missing), spot))
        if not second:
            rough = friction_of(source)
            tiles.append(
                jnp.where(
                    everywhere(missing),
                    row_roll(rough, near - side),
                    row_roll(rough, near - opposite[side]),
                )
            )
        return tiles

    for p in range(per_dev):
        patch = held_patches[p]
        for side, spot, near in ((WEST, 0, 1), (EAST, 6, 6)):
            group = 2 * p + side
            for f, tile in enumerate(by_field(patch, side, spot, near)):
                turned[f, group * SUB : (group + 1) * SUB] = tile
        for end, side, spot, near in ((0, SOUTH, 6, 7), (1, NORTH, 0, 0)):
            for f, tile in enumerate(by_field(patch, side, spot, near)):
                halo[p, end, f] = tile

    for f in range(held_fields):
        turned[f] = turned[f].T

    group_lane = lanes % SUB
    odd_group = (lanes // SUB) % 2
    from_halo = ((odd_group == 0) & (group_lane < 2)) | ((odd_group == 1) & (group_lane >= 6))

    def fill_strip(k, _):
        for f in range(held_fields):
            strip_a[f, chunk(k + 1), :] = jnp.where(
                from_halo, turned[f, chunk(k), :], own_strip[f, chunk(k), :]
            )
        return 0

    lax.fori_loop(0, chunks, fill_strip, 0, unroll=2)

    for end, side, row, line in ((0, SOUTH, 7, 1), (1, NORTH, 0, 0)):
        place = slice(0, SUB) if end == 0 else slice((chunks + 1) * SUB, (chunks + 2) * SUB)
        corner = [
            lay_strip([halo[p, end, f] for p in range(per_dev)]) for f in range(held_fields)
        ]
        for p in range(per_dev):
            patch = held_patches[p]
            beyond = neighbors[side, patch]
            missing = beyond < 0
            base = jnp.where(missing, patch, beyond)
            edge = jnp.where(missing, side, opposite[side])
            for across, spot, inner, outer in ((WEST, 1, 0, LANES - 1), (EAST, 6, LANES - 1, 0)):
                aside = neighbors[across, base]
                alone = everywhere(aside < 0)
                source = spot_of(jnp.where(aside < 0, base, aside))
                lane = (2 * p + across) * SUB + spot
                flow = repaired(tile_of(source, edge), side, missing)
                bed = bed_lines(source, side, missing)
                flow = jnp.where(alone, lane_roll(flow, lane - inner), lane_roll(flow, lane - outer))
                bed = jnp.where(alone, lane_roll(bed, lane - inner), lane_roll(bed, lane - outer))
                here = (lanes == lane) & (rows == row)
                for f in range(4):
                    corner[f] = jnp.where(here, row_roll(flow, row - 2 * f - line), corner[f])
                corner[4] = jnp.where(here, row_roll(bed, row - line), corner[4])
        for f in range(held_fields):
            strip_a[f, place, :] = corner[f]

    for p in range(per_dev):
        for f in range(held_fields):
            rows_a[2 * p, f] = jnp.where(
                rows < 2, row_roll(halo[p, 0, f], 2), row_roll(edges[p, 0, f], 2)
            )
            rows_a[2 * p + 1, f] = jnp.where(
                rows >= 6, row_roll(halo[p, 1, f], 6), row_roll(edges[p, 1, f], -2)
            )

    if not second:
        rough_strip[...] = strip_a[5]
        for i in range(2 * per_dev):
            rough_rows[i] = rows_a[i, 5]

    def run(source, target):
        def load(f, k):
            return rough_strip[chunk(k), :] if f == 5 else source[f, chunk(k), :]

        def store(f, k, value):
            target[f, chunk(k), :] = value

        advance_rows(load, store, chunks + 2, 2)

    run(strip_a, strip_b)
    run(strip_b, strip_a)

    def row_strip(i, _):
        def step(source, target):
            def load(f, k):
                return rough_rows[i] if f == 5 else source[i, f]

            def store(f, k, value):
                target[i, f] = value

            advance_rows(load, store, 1, 1)

        step(rows_a, rows_b)
        step(rows_b, rows_a)
        return 0

    lax.fori_loop(0, 2 * per_dev, row_strip, 0, unroll=2)

    ends = slots if second else list(range(per_dev))

    def merge(k, _):
        for f in range(5):
            strip = strip_a[f, chunk(k + 1), :]
            for p in range(per_dev):
                value = main[p, f, chunk(k), :]
                value = jnp.where(
                    (rows < 2) & everywhere(k == 0), row_roll(rows_a[2 * p, f], -2), value
                )
                value = jnp.where(
                    (rows >= 6) & everywhere(k == chunks - 1),
                    row_roll(rows_a[2 * p + 1, f], 2),
                    value,
                )
                west = lane_roll(strip, -(2 * p * SUB + 2))
                east = lane_roll(strip, -6 - (2 * p + 1) * SUB)
                value = jnp.where(lanes < 2, west, value)
                ended[ends[p], f, chunk(k), :] = jnp.where(lanes >= LANES - 2, east, value)
        for p in range(per_dev):
            ended[ends[p], 5, chunk(k), :] = main[p, 5, chunk(k), :]
        return 0

    lax.fori_loop(0, chunks, merge, 0)
    if not second:
        pack_frames(ended, frames, turned.at[0], False)


def finish_round(device, neighbors, migration, pieces, count, rough):
    pool, main, strip, edges = pieces
    second = rough is not None
    per_dev, _, extent, _ = main.shape

    def shape(*sizes):
        return jax.ShapeDtypeStruct(sizes, jnp.float32)

    rough_shapes = (shape(extent + 2 * SUB, LANES), shape(2 * per_dev, SUB, LANES))
    out_shape = (shape(*main.shape),)
    if not second:
        out_shape += (shape(per_dev * PATCH_TILES, SUB, LANES),) + rough_shapes
    operands = (device, neighbors, migration, main, strip, edges, pool)
    if second:
        operands += rough
    return pl.pallas_call(
        functools.partial(step_kernel, count, second),
        out_shape=out_shape,
        in_specs=[SMEM] * 3 + [VMEM] * (len(operands) - 3),
        out_specs=(VMEM,) * len(out_shape),
        scratch_shapes=[
            pltpu.VMEM((6, extent + 2 * SUB, LANES), jnp.float32),
            pltpu.VMEM((6, extent + 2 * SUB, LANES), jnp.float32),
            pltpu.VMEM((2 * per_dev, 6, SUB, LANES), jnp.float32),
            pltpu.VMEM((2 * per_dev, 6, SUB, LANES), jnp.float32),
            pltpu.VMEM((6, LANES, LANES), jnp.float32),
            pltpu.VMEM((per_dev, 2, 6, SUB, LANES), jnp.float32),
        ],
        compiler_params=pltpu.CompilerParams(vmem_limit_bytes=VMEM_LIMIT),
    )(*operands)


def shards(fields, wet_mask, neighbors, migration):
    count = lax.axis_size("curve")
    moves = migration.shape[1]
    device = lax.axis_index("curve").astype(jnp.int32).reshape(1)
    neighbors, migration = neighbors.T, migration.T
    started, frames = begin(device, migration, fields, wet_mask)
    pieces = gather_frames(started, frames, count, moves, 0)
    halfway, frames, *rough = finish_round(device, neighbors, migration, pieces, count, None)
    pieces = gather_frames(halfway, frames, count, 0, 1)
    (ended,) = finish_round(device, neighbors, migration, pieces, count, tuple(rough))
    return ended


def solution(mesh):
    placed = (P("curve", None, None, None), P("curve", None, None), P(), P())
    return jax.shard_map(
        shards, mesh=mesh, in_specs=placed, out_specs=P("curve", None, None, None), check_vma=False
    )
```

```python
import functools

import jax
import jax.numpy as jnp
from jax import lax
from jax.experimental import pallas as pl
from jax.experimental.pallas import tpu as pltpu
from jax.sharding import PartitionSpec as P

GRAVITY = 9.81
TIME_STEP = 0.04
DRY_EPS = 0.01
CAPACITY = 0.02
EROSION = 0.5
SETTLING = 0.2
POROSITY = 0.4

LANES = 128
SUB = 8
WEST, EAST, SOUTH, NORTH = range(4)
BED_TILE, PATCH_TILES = 4, 5
VMEM_LIMIT = 48 * 1024 * 1024
VMEM = pl.BlockSpec(memory_space=pltpu.VMEM)
SMEM = pl.BlockSpec(memory_space=pltpu.SMEM)
ANY = pl.BlockSpec(memory_space=pl.ANY)


def lane_index():
    return lax.broadcasted_iota(jnp.int32, (SUB, LANES), 1)


def row_index():
    return lax.broadcasted_iota(jnp.int32, (SUB, LANES), 0)


def lane_roll(value, shift):
    shift = shift % LANES
    return value if shift == 0 else pltpu.roll(value, shift, 1)


def row_roll(value, shift):
    shift = shift % SUB
    return value if shift == 0 else pltpu.roll(value, shift, 0)


def everywhere(flag):
    return jnp.full((SUB, LANES), flag.astype(jnp.int32)) > 0


def inverse_of(value):
    rough = pl.reciprocal(value, approx=True)
    return rough * (2.0 - value * rough)


def root_of(value):
    return value * lax.rsqrt(jnp.maximum(value, 1e-30))


def cell_terms(h, qx, qy, m):
    inverse = h * inverse_of(h * h + DRY_EPS)
    wet = jnp.maximum(h, 0.0)
    return (h, qx, qy, m, qx * inverse, qy * inverse, m * inverse, root_of(wet + 0.01))


def doubled_flux(left, right):
    h0, n0, t0, m0, u0, w0, s0, r0 = left
    h1, n1, t1, m1, u1, w1, s1, r1 = right
    scale = inverse_of(r0 + r1)
    part0 = r0 * scale
    part1 = r1 * scale
    mean_u = part0 * u0 + part1 * u1
    mean_w = part0 * w0 + part1 * w1
    mean_s = part0 * s0 + part1 * s1
    celerity = root_of((0.5 * GRAVITY) * (jnp.maximum(h0, 0.0) + jnp.maximum(h1, 0.0))) + 0.1
    half = 0.5 * inverse_of(celerity)
    dh = h1 - h0
    dn = n1 - n0
    plus = mean_u + celerity
    minus = mean_u - celerity
    p1 = jnp.abs(minus) * ((plus * dh - dn) * half)
    p3 = jnp.abs(plus) * ((dn - minus * dh) * half)
    both = p1 + p3
    middle = jnp.abs(mean_u)
    return (
        n0 + n1 - both,
        n0 * u0 + n1 * u1 + (0.5 * GRAVITY) * (h0 * h0 + h1 * h1) - (p1 * minus + p3 * plus),
        n0 * w0 + n1 * w1 - (both * mean_w + middle * (t1 - t0 - mean_w * dh)),
        n0 * s0 + n1 * s1 - (both * mean_s + middle * (m1 - m0 - mean_s * dh)),
    )


def swapped(cell):
    h, qx, qy, m, u, v, s, r = cell
    return (h, qy, qx, m, v, u, s, r)


def advance_rows(load, store, count, unroll, slices=1, pause=None):
    rows = row_index()
    first, last = rows == 0, rows == SUB - 1

    def upper(now, after):
        return row_roll(jnp.where(first, after, now), -1)

    def lower(before_rolled, rolled):
        return jnp.where(first, before_rolled, rolled)

    def fetch(k):
        return cell_terms(load(0, k), load(1, k), load(2, k), load(3, k)) + (load(4, k),)

    def body(k, carry):
        now, flux_before, bed_before = carry
        after = fetch(jnp.minimum(k + 1, count - 1)) if count > 1 else now
        cell, bed = now[:8], now[8]
        up = tuple(upper(a, b) for a, b in zip(cell, after[:8]))
        y_flux = doubled_flux(swapped(cell), swapped(up))
        y_rolled = tuple(row_roll(f, 1) for f in y_flux)
        dy = tuple(f - lower(b, r) for f, b, r in zip(y_flux, flux_before, y_rolled))
        west = tuple(lane_roll(a, 1) for a in cell)
        x_flux = doubled_flux(west, cell)
        dx = tuple(lane_roll(f, -1) - f for f in x_flux)
        bed_rolled = row_roll(bed, 1)
        bed_y = upper(bed, after[8]) - lower(bed_before, bed_rolled)
        bed_x = lane_roll(bed, -1) - lane_roll(bed, 1)
        h, qx, qy, m = cell[:4]
        friction = load(5, k)
        step = 0.5 * TIME_STEP
        slope = (step * GRAVITY) * h
        new_h = h - step * (dx[0] + dy[0])
        new_x = qx - step * (dx[1] + dy[2]) - slope * bed_x
        new_y = qy - step * (dx[2] + dy[1]) - slope * bed_y
        new_m = m - step * (dx[3] + dy[3])
        inverse = new_h * inverse_of(new_h * new_h + DRY_EPS)
        speed_x = new_x * inverse
        speed_y = new_y * inverse
        square = speed_x * speed_x + speed_y * speed_y
        speed = root_of(square)
        depth = jnp.maximum(new_h, 0.0) + 0.1
        factor = depth * inverse_of(depth + TIME_STEP * friction * speed)
        conc = new_m * inverse
        net = EROSION * jnp.maximum(CAPACITY * square - conc, 0.0) - SETTLING * conc
        store(0, k, new_h)
        store(1, k, new_x * factor)
        store(2, k, new_y * factor)
        store(3, k, new_m + TIME_STEP * net)
        store(4, k, bed - (TIME_STEP / (1.0 - POROSITY)) * net)
        return after, y_rolled, bed_rolled

    zero = jnp.zeros((SUB, LANES), jnp.float32)
    start = (fetch(0), (zero,) * 4, zero)
    if count == 1:
        body(0, start)
    else:
        each = count // slices
        for part in range(slices):
            start = lax.fori_loop(part * each, (part + 1) * each, body, start, unroll=unroll)
            if pause is not None:
                pause(part)


def chunk(k):
    return pl.ds(pl.multiple_of(k * SUB, SUB), SUB)


def pack_frames(patches, frames, turned, with_friction):
    per_dev, _, extent, _ = patches.shape
    fields = 6 if with_friction else 5
    lanes = lane_index()

    def columns(k, _):
        total = jnp.zeros((SUB, LANES), jnp.float32)
        for p in range(per_dev):
            for f in range(fields):
                value = patches[p, f, chunk(k), :]
                base = p * 32
                if f < 4:
                    spots = ((base + 2 * f, 2, 0), (base + 8 + 2 * f, 2, LANES - 2))
                elif f == 4:
                    spots = ((base + 16, 2, 0), (base + 18, 2, LANES - 2))
                else:
                    spots = ((base + 24, 1, 0), (base + 25, 1, LANES - 1))
                for spot, width, origin in spots:
                    inside = (lanes >= spot) & (lanes < spot + width)
                    total = jnp.where(inside, lane_roll(value, spot - origin), total)
        turned[chunk(k), :] = total
        return 0

    lax.fori_loop(0, extent // SUB, columns, 0, unroll=2)
    turned[...] = turned[...].T
    rows = row_index()
    low, high = slice(0, SUB), slice(extent - SUB, extent)
    for p in range(per_dev):
        base = p * 32
        out = frames.at[pl.ds(p * PATCH_TILES, PATCH_TILES)]
        out[WEST] = turned[base : base + 8]
        out[EAST] = turned[base + 8 : base + 16]
        south = north = jnp.zeros((SUB, LANES), jnp.float32)
        for f in range(4):
            inside = (rows >= 2 * f) & (rows < 2 * f + 2)
            south = jnp.where(inside, row_roll(patches[p, f, low, :], 2 * f), south)
            north = jnp.where(inside, row_roll(patches[p, f, high, :], 2 * f + 2), north)
        out[SOUTH] = south
        out[NORTH] = north
        bed = turned[base + 16 : base + 24]
        bed = jnp.where((rows == 4) | (rows == 5), row_roll(patches[p, 4, low, :], 4), bed)
        bed = jnp.where(rows >= 6, patches[p, 4, high, :], bed)
        out[BED_TILE] = bed
        if with_friction:
            rough = turned[base + 24 : base + 32]
            rough = jnp.where(rows == 2, row_roll(patches[p, 5, low, :], 2), rough)
            rough = jnp.where(rows == 3, row_roll(patches[p, 5, high, :], 4), rough)
            if p % 2 == 0:
                paired = rough
            else:
                paired = jnp.where(rows < 4, paired, row_roll(rough, 4))
            if p % 2 == 1 or p == per_dev - 1:
                frames[per_dev * PATCH_TILES + p // 2] = paired


def kept_slots(migration, owner, per_dev):
    moves = migration.shape[0]
    rank = jnp.int32(0)
    slots = [jnp.int32(0)] * (per_dev - moves)
    for slot in range(per_dev):
        stays = jnp.int32(1)
        for k in range(moves):
            stays = stays * jnp.where(migration[k, owner] == slot, 0, 1)
        for j in range(per_dev - moves):
            slots[j] = jnp.where((stays == 1) & (rank == j), slot, slots[j])
        rank = rank + stays
    return slots + [migration[k, owner] for k in range(moves)]


def begin_kernel(device, migration, fields, mask, started, frames, turned):
    per_dev = fields.shape[0]
    slots = kept_slots(migration, device[0], per_dev)
    for p, slot in enumerate(slots):
        wet = mask[slot].astype(jnp.float32)
        for f in range(6):
            started[p, f] = fields[slot, f] * wet if f < 4 else fields[slot, f]
    pack_frames(started, frames, turned, True)


def begin(device, migration, fields, mask):
    per_dev = fields.shape[0]
    return pl.pallas_call(
        begin_kernel,
        out_shape=(
            jax.ShapeDtypeStruct(fields.shape, jnp.float32),
            jax.ShapeDtypeStruct(
                (per_dev * PATCH_TILES + (per_dev + 1) // 2, SUB, LANES), jnp.float32
            ),
        ),
        in_specs=[SMEM, SMEM, VMEM, VMEM],
        out_specs=(VMEM, VMEM),
        scratch_shapes=[pltpu.VMEM((LANES, LANES), jnp.float32)],
        compiler_params=pltpu.CompilerParams(vmem_limit_bytes=VMEM_LIMIT),
    )(device, migration, fields, mask)


def gather_kernel(
    count, moves, patches, mine, pool, main, strip, edges,
    held, middle, own_sem, held_sem, move_send, move_recv, send_sem, recv_sem,
):
    per_dev, _, extent, _ = patches.shape
    chunks = extent // SUB
    length = count // 8
    me = lax.axis_index("curve")
    core, x, y, z = me % 2, (me // 2) % 2, (me // 4) % 2, me // 8
    other_core = me + 1 - 2 * core
    other_x = me + 2 - 4 * x
    other_y = me + 4 - 8 * y
    across = me + 6 - 4 * x - 8 * y
    column = []
    for distance in range(1, length):
        for there, device in ((z >= distance, me - 8 * distance),
                              (z + distance < length, me + 8 * distance)):
            column.append((jnp.where(there, device, other_core), there))
    following = lax.rem(me + 1, count)
    previous = lax.rem(me + count - 1, count)

    local = []
    for p in range(per_dev - moves):
        local.append(pltpu.make_async_copy(patches.at[p], held.at[p], held_sem.at[p]))
        local[p].start()
    tiles = mine.shape[0]
    own_copy = pltpu.make_async_copy(mine, pool.at[pl.ds(me * tiles, tiles)], own_sem)
    own_copy.start()

    barrier = pltpu.get_barrier_semaphore()

    def greet(device):
        pl.semaphore_signal(
            barrier, inc=1, device_id=(device,), device_id_type=pl.DeviceIdType.MESH
        )

    friends = [other_core, other_x, other_y] + ([following, previous] if moves else [])
    for device in friends:
        greet(device)
    for device, there in column:
        pl.when(there)(functools.partial(greet, device))
    pl.semaphore_wait(barrier, len(friends) + length - 1)

    def copy_of(block, device, slot, own):
        target = pool.at[pl.ds(block * tiles, tiles)]
        return pltpu.make_async_remote_copy(
            src_ref=mine if own else target,
            dst_ref=target,
            send_sem=send_sem.at[slot],
            recv_sem=recv_sem.at[block],
            device_id=(device,),
            device_id_type=pl.DeviceIdType.MESH,
        )

    def both(first, second):
        if first is None:
            return second
        return first if second is None else first & second

    def perform(when, action):
        if when is None:
            action()
        else:
            pl.when(when)(action)

    sends = []
    events = {}

    def send(at, block, device, when=None, own=False):
        slot = len(sends)
        sends.append((block, device, slot, own, when))

        def action():
            perform(when, lambda: copy_of(block, device, slot, own).start())

        events.setdefault(at, []).append(action)

    def arrive(at, block, when=None):
        def action():
            perform(when, lambda: copy_of(block, other_core, 0, False).wait_recv())

        events.setdefault(at, []).append(action)

    for device in (other_x, other_y):
        send(-1, me, device, None, True)
    for device, there in column:
        send(-1, me, device, there, True)
    send(-1, me, other_core, None, True)

    def beside(at, level, when):
        x_block = level * 8 + other_x % 8
        y_block = level * 8 + other_y % 8
        for block, turn, device in (
            (x_block, level % 2 == 0, other_y), (y_block, level % 2 == 1, other_x)
        ):
            arrive(at, block, when)
            send(at, block, device, both(turn, when))
            send(at, block, other_core, when)

    for distance in range(length):
        places = [(z, None)]
        if distance:
            places = [(z - distance, z >= distance), (z + distance, z + distance < length)]
        for level, there in places:
            if distance:
                block = level * 8 + me % 8
                at = 2 * distance + 2
                arrive(at, block, there)
                for device in (other_x, other_y, other_core):
                    send(at, block, device, there)
            beside(4 * distance + 6 if distance else 4, level, there)
            block = level * 8 + across % 8
            arrive(4 * distance + 10, block, there)
            send(4 * distance + 10, block, other_core, there)

    def occur(at):
        for action in events.get(at, ()):
            action()

    occur(-1)
    moving = []
    for k in range(moves):
        moving.append(
            pltpu.make_async_remote_copy(
                src_ref=patches.at[per_dev - moves + k],
                dst_ref=held.at[per_dev - moves + k],
                send_sem=move_send.at[k],
                recv_sem=move_recv.at[k],
                device_id=(following,),
                device_id_type=pl.DeviceIdType.MESH,
            )
        )
        moving[k].start()

    slices = 4
    for copy in local:
        copy.wait()

    def main_patch(p, _):
        for k in range(moves):
            pl.when(p == per_dev - moves + k)(moving[k].wait_recv)
        start, end = held.at[p], main.at[p]
        for step, (source, target) in enumerate(((start, middle), (middle, end))):

            def load(f, k):
                return (start if f == 5 else source)[f, chunk(k), :]

            def store(f, k, value):
                target[f, chunk(k), :] = value

            def pause(part):
                for q in range(per_dev):
                    pl.when(p == q)(lambda: occur(q * 2 * slices + step * slices + part))

            advance_rows(load, store, chunks, 4, slices, pause)
        end[5] = start[5]
        return 0

    lax.fori_loop(0, per_dev, main_patch, 0)

    def fill_strip(k, _):
        for f in range(6):
            strip[f, chunk(k), :] = lay_strip([held[p, f, chunk(k), :] for p in range(per_dev)])
        return 0

    lax.fori_loop(0, chunks, fill_strip, 0, unroll=2)
    for p in range(per_dev):
        for f in range(6):
            edges[p, 0, f] = held[p, f, 0:SUB, :]
            edges[p, 1, f] = held[p, f, extent - SUB : extent, :]

    for at in sorted(events):
        if at >= 2 * slices * per_dev:
            occur(at)
    for square in range(4):
        for level in range(length):
            copy_of(level * 8 + 2 * square + other_core % 2, other_core, 0, False).wait_recv()
    own_copy.wait()
    for copy in moving:
        copy.wait_send()
    for block, device, slot, own, when in sends:
        perform(when, copy_of(block, device, slot, own).wait_send)


def lay_strip(values):
    lanes = lane_index()
    total = jnp.zeros((SUB, LANES), jnp.float32)
    for p, value in enumerate(values):
        for side, shift in ((WEST, 2), (EAST, 6)):
            group = 2 * p + side
            total = jnp.where(lanes // SUB == group, lane_roll(value, group * SUB + shift), total)
    return total


def gather_frames(patches, frames, count, moves, collective_id):
    per_dev, _, extent, _ = patches.shape

    def shape(*sizes):
        return jax.ShapeDtypeStruct(sizes, jnp.float32)

    return pl.pallas_call(
        functools.partial(gather_kernel, count, moves),
        out_shape=(
            shape(count * frames.shape[0], *frames.shape[1:]),
            shape(*patches.shape),
            shape(6, extent, LANES),
            shape(per_dev, 2, 6, SUB, LANES),
        ),
        in_specs=[ANY, ANY],
        out_specs=(VMEM, VMEM, VMEM, VMEM),
        scratch_shapes=[
            pltpu.VMEM(patches.shape, jnp.float32),
            pltpu.VMEM((6, extent, LANES), jnp.float32),
            pltpu.SemaphoreType.DMA,
            pltpu.SemaphoreType.DMA((per_dev,)),
            pltpu.SemaphoreType.DMA((max(moves, 1),)),
            pltpu.SemaphoreType.DMA((max(moves, 1),)),
            pltpu.SemaphoreType.DMA((5 * count,)),
            pltpu.SemaphoreType.DMA((count,)),
        ],
        compiler_params=pltpu.CompilerParams(
            collective_id=collective_id, has_side_effects=True, vmem_limit_bytes=VMEM_LIMIT
        ),
    )(patches, frames)


def step_kernel(count, second, device, neighbors, migration, main, own_strip, edges, pool, *refs):
    if second:
        rough_strip, rough_rows, ended, strip_a, strip_b, rows_a, rows_b, turned, halo = refs
    else:
        (ended, frames, rough_strip, rough_rows) = refs[:4]
        (strip_a, strip_b, rows_a, rows_b, turned, halo) = refs[4:]
    held_fields = 5 if second else 6
    per_dev, _, extent, _ = main.shape
    chunks = extent // SUB
    moves = migration.shape[0]
    owner = device[0]
    lanes, rows = lane_index(), row_index()

    def ring(value):
        return jnp.where(value < 0, value + count, jnp.where(value >= count, value - count, value))

    slots = kept_slots(migration, owner, per_dev)
    before = ring(owner - 1)
    held_patches = [owner * per_dev + slot for slot in slots[: per_dev - moves]]
    held_patches += [before * per_dev + migration[k, before] for k in range(moves)]

    tiles = pool.shape[0] // count

    def spot_of(patch):
        home = patch // per_dev
        slot = patch - home * per_dev
        block, place = home, slot
        for k in range(moves):
            place = place - jnp.where(migration[k, home] < slot, 1, 0)
        for k in range(moves):
            here = migration[k, home] == slot
            place = jnp.where(here, per_dev - moves + k, place)
            if second:
                block = jnp.where(here, ring(home + 1), block)
        return block, place

    def tile_of(spot, tile):
        return pool[spot[0] * tiles + spot[1] * PATCH_TILES + tile]

    def friction_of(spot):
        tile = pool[spot[0] * tiles + per_dev * PATCH_TILES + spot[1] // 2]
        return jnp.where(everywhere(spot[1] % 2 == 1), row_roll(tile, 4), tile)

    opposite = {WEST: EAST, EAST: WEST, SOUTH: NORTH, NORTH: SOUTH}

    def repaired(tile, side, missing):
        if side in (WEST, SOUTH):
            return jnp.where(everywhere(missing) & (rows % 2 == 1), row_roll(tile, 1), tile)
        return jnp.where(everywhere(missing) & (rows % 2 == 0), row_roll(tile, -1), tile)

    def bed_lines(source, side, missing):
        bed = tile_of(source, BED_TILE)
        bed = jnp.where(
            everywhere(missing), row_roll(bed, -2 * side), row_roll(bed, -2 * opposite[side])
        )
        return repaired(bed, side, missing)

    def by_field(patch, side, spot, near):
        beyond = neighbors[side, patch]
        missing = beyond < 0
        source = spot_of(jnp.where(missing, patch, beyond))
        edge = jnp.where(missing, side, opposite[side])
        flow = repaired(tile_of(source, edge), side, missing)
        tiles = [row_roll(flow, spot - 2 * f) for f in range(4)]
        tiles.append(row_roll(bed_lines(source, side, missing), spot))
        if not second:
            rough = friction_of(source)
            tiles.append(
                jnp.where(
                    everywhere(missing),
                    row_roll(rough, near - side),
                    row_roll(rough, near - opposite[side]),
                )
            )
        return tiles

    for p in range(per_dev):
        patch = held_patches[p]
        for side, spot, near in ((WEST, 0, 1), (EAST, 6, 6)):
            group = 2 * p + side
            for f, tile in enumerate(by_field(patch, side, spot, near)):
                turned[f, group * SUB : (group + 1) * SUB] = tile
        for end, side, spot, near in ((0, SOUTH, 6, 7), (1, NORTH, 0, 0)):
            for f, tile in enumerate(by_field(patch, side, spot, near)):
                halo[p, end, f] = tile

    for f in range(held_fields):
        turned[f] = turned[f].T

    group_lane = lanes % SUB
    odd_group = (lanes // SUB) % 2
    from_halo = ((odd_group == 0) & (group_lane < 2)) | ((odd_group == 1) & (group_lane >= 6))

    def fill_strip(k, _):
        for f in range(held_fields):
            strip_a[f, chunk(k + 1), :] = jnp.where(
                from_halo, turned[f, chunk(k), :], own_strip[f, chunk(k), :]
            )
        return 0

    lax.fori_loop(0, chunks, fill_strip, 0, unroll=2)

    for end, side, row, line in ((0, SOUTH, 7, 1), (1, NORTH, 0, 0)):
        place = slice(0, SUB) if end == 0 else slice((chunks + 1) * SUB, (chunks + 2) * SUB)
        corner = [
            lay_strip([halo[p, end, f] for p in range(per_dev)]) for f in range(held_fields)
        ]
        for p in range(per_dev):
            patch = held_patches[p]
            beyond = neighbors[side, patch]
            missing = beyond < 0
            base = jnp.where(missing, patch, beyond)
            edge = jnp.where(missing, side, opposite[side])
            for across, spot, inner, outer in ((WEST, 1, 0, LANES - 1), (EAST, 6, LANES - 1, 0)):
                aside = neighbors[across, base]
                alone = everywhere(aside < 0)
                source = spot_of(jnp.where(aside < 0, base, aside))
                lane = (2 * p + across) * SUB + spot
                flow = repaired(tile_of(source, edge), side, missing)
                bed = bed_lines(source, side, missing)
                flow = jnp.where(alone, lane_roll(flow, lane - inner), lane_roll(flow, lane - outer))
                bed = jnp.where(alone, lane_roll(bed, lane - inner), lane_roll(bed, lane - outer))
                here = (lanes == lane) & (rows == row)
                for f in range(4):
                    corner[f] = jnp.where(here, row_roll(flow, row - 2 * f - line), corner[f])
                corner[4] = jnp.where(here, row_roll(bed, row - line), corner[4])
        for f in range(held_fields):
            strip_a[f, place, :] = corner[f]

    for p in range(per_dev):
        for f in range(held_fields):
            rows_a[2 * p, f] = jnp.where(
                rows < 2, row_roll(halo[p, 0, f], 2), row_roll(edges[p, 0, f], 2)
            )
            rows_a[2 * p + 1, f] = jnp.where(
                rows >= 6, row_roll(halo[p, 1, f], 6), row_roll(edges[p, 1, f], -2)
            )

    if not second:
        rough_strip[...] = strip_a[5]
        for i in range(2 * per_dev):
            rough_rows[i] = rows_a[i, 5]

    def run(source, target):
        def load(f, k):
            return rough_strip[chunk(k), :] if f == 5 else source[f, chunk(k), :]

        def store(f, k, value):
            target[f, chunk(k), :] = value

        advance_rows(load, store, chunks + 2, 2)

    run(strip_a, strip_b)
    run(strip_b, strip_a)

    def row_strip(i, _):
        def step(source, target):
            def load(f, k):
                return rough_rows[i] if f == 5 else source[i, f]

            def store(f, k, value):
                target[i, f] = value

            advance_rows(load, store, 1, 1)

        step(rows_a, rows_b)
        step(rows_b, rows_a)
        return 0

    lax.fori_loop(0, 2 * per_dev, row_strip, 0, unroll=2)

    ends = slots if second else list(range(per_dev))

    def merge(k, _):
        for f in range(5):
            strip = strip_a[f, chunk(k + 1), :]
            for p in range(per_dev):
                value = main[p, f, chunk(k), :]
                value = jnp.where(
                    (rows < 2) & everywhere(k == 0), row_roll(rows_a[2 * p, f], -2), value
                )
                value = jnp.where(
                    (rows >= 6) & everywhere(k == chunks - 1),
                    row_roll(rows_a[2 * p + 1, f], 2),
                    value,
                )
                west = lane_roll(strip, -(2 * p * SUB + 2))
                east = lane_roll(strip, -6 - (2 * p + 1) * SUB)
                value = jnp.where(lanes < 2, west, value)
                ended[ends[p], f, chunk(k), :] = jnp.where(lanes >= LANES - 2, east, value)
        for p in range(per_dev):
            ended[ends[p], 5, chunk(k), :] = main[p, 5, chunk(k), :]
        return 0

    lax.fori_loop(0, chunks, merge, 0)
    if not second:
        pack_frames(ended, frames, turned.at[0], False)


def finish_round(device, neighbors, migration, pieces, count, rough):
    pool, main, strip, edges = pieces
    second = rough is not None
    per_dev, _, extent, _ = main.shape

    def shape(*sizes):
        return jax.ShapeDtypeStruct(sizes, jnp.float32)

    rough_shapes = (shape(extent + 2 * SUB, LANES), shape(2 * per_dev, SUB, LANES))
    out_shape = (shape(*main.shape),)
    if not second:
        out_shape += (shape(per_dev * PATCH_TILES, SUB, LANES),) + rough_shapes
    operands = (device, neighbors, migration, main, strip, edges, pool)
    if second:
        operands += rough
    return pl.pallas_call(
        functools.partial(step_kernel, count, second),
        out_shape=out_shape,
        in_specs=[SMEM] * 3 + [VMEM] * (len(operands) - 3),
        out_specs=(VMEM,) * len(out_shape),
        scratch_shapes=[
            pltpu.VMEM((6, extent + 2 * SUB, LANES), jnp.float32),
            pltpu.VMEM((6, extent + 2 * SUB, LANES), jnp.float32),
            pltpu.VMEM((2 * per_dev, 6, SUB, LANES), jnp.float32),
            pltpu.VMEM((2 * per_dev, 6, SUB, LANES), jnp.float32),
            pltpu.VMEM((6, LANES, LANES), jnp.float32),
            pltpu.VMEM((per_dev, 2, 6, SUB, LANES), jnp.float32),
        ],
        compiler_params=pltpu.CompilerParams(vmem_limit_bytes=VMEM_LIMIT),
    )(*operands)


def shards(fields, wet_mask, neighbors, migration):
    count = lax.axis_size("curve")
    moves = migration.shape[1]
    device = lax.axis_index("curve").astype(jnp.int32).reshape(1)
    neighbors, migration = neighbors.T, migration.T
    started, frames = begin(device, migration, fields, wet_mask)
    pieces = gather_frames(started, frames, count, moves, 0)
    halfway, frames, *rough = finish_round(device, neighbors, migration, pieces, count, None)
    pieces = gather_frames(halfway, frames, count, 0, 1)
    (ended,) = finish_round(device, neighbors, migration, pieces, count, tuple(rough))
    return ended


def solution(mesh):
    placed = (P("curve", None, None, None), P("curve", None, None), P(), P())
    return jax.shard_map(
        shards, mesh=mesh, in_specs=placed, out_specs=P("curve", None, None, None), check_vma=False
    )
```

```python
import functools

import jax
import jax.numpy as jnp
from jax import lax
from jax.experimental import pallas as pl
from jax.experimental.pallas import tpu as pltpu
from jax.sharding import PartitionSpec as P

GRAVITY = 9.81
TIME_STEP = 0.04
DRY_EPS = 0.01
CAPACITY = 0.02
EROSION = 0.5
SETTLING = 0.2
POROSITY = 0.4

LANES = 128
SUB = 8
WEST, EAST, SOUTH, NORTH = range(4)
BED_TILE, PATCH_TILES = 4, 5
VMEM_LIMIT = 48 * 1024 * 1024
VMEM = pl.BlockSpec(memory_space=pltpu.VMEM)
SMEM = pl.BlockSpec(memory_space=pltpu.SMEM)
ANY = pl.BlockSpec(memory_space=pl.ANY)


def lane_index():
    return lax.broadcasted_iota(jnp.int32, (SUB, LANES), 1)


def row_index():
    return lax.broadcasted_iota(jnp.int32, (SUB, LANES), 0)


def lane_roll(value, shift):
    shift = shift % LANES
    return value if shift == 0 else pltpu.roll(value, shift, 1)


def row_roll(value, shift):
    shift = shift % SUB
    return value if shift == 0 else pltpu.roll(value, shift, 0)


def everywhere(flag):
    return jnp.full((SUB, LANES), flag.astype(jnp.int32)) > 0


def inverse_of(value):
    rough = pl.reciprocal(value, approx=True)
    return rough * (2.0 - value * rough)


def root_of(value):
    return value * lax.rsqrt(jnp.maximum(value, 1e-30))


def cell_terms(h, qx, qy, m):
    inverse = h * inverse_of(h * h + DRY_EPS)
    wet = jnp.maximum(h, 0.0)
    return (h, qx, qy, m, qx * inverse, qy * inverse, m * inverse, root_of(wet + 0.01))


def doubled_flux(left, right):
    h0, n0, t0, m0, u0, w0, s0, r0 = left
    h1, n1, t1, m1, u1, w1, s1, r1 = right
    scale = inverse_of(r0 + r1)
    part0 = r0 * scale
    part1 = r1 * scale
    mean_u = part0 * u0 + part1 * u1
    mean_w = part0 * w0 + part1 * w1
    mean_s = part0 * s0 + part1 * s1
    celerity = root_of((0.5 * GRAVITY) * (jnp.maximum(h0, 0.0) + jnp.maximum(h1, 0.0))) + 0.1
    half = 0.5 * inverse_of(celerity)
    dh = h1 - h0
    dn = n1 - n0
    plus = mean_u + celerity
    minus = mean_u - celerity
    p1 = jnp.abs(minus) * ((plus * dh - dn) * half)
    p3 = jnp.abs(plus) * ((dn - minus * dh) * half)
    both = p1 + p3
    middle = jnp.abs(mean_u)
    return (
        n0 + n1 - both,
        n0 * u0 + n1 * u1 + (0.5 * GRAVITY) * (h0 * h0 + h1 * h1) - (p1 * minus + p3 * plus),
        n0 * w0 + n1 * w1 - (both * mean_w + middle * (t1 - t0 - mean_w * dh)),
        n0 * s0 + n1 * s1 - (both * mean_s + middle * (m1 - m0 - mean_s * dh)),
    )


def swapped(cell):
    h, qx, qy, m, u, v, s, r = cell
    return (h, qy, qx, m, v, u, s, r)


def advance_rows(load, store, count, unroll, slices=1, pause=None):
    rows = row_index()
    first, last = rows == 0, rows == SUB - 1

    def upper(now, after):
        return row_roll(jnp.where(first, after, now), -1)

    def lower(before_rolled, rolled):
        return jnp.where(first, before_rolled, rolled)

    def fetch(k):
        return cell_terms(load(0, k), load(1, k), load(2, k), load(3, k)) + (load(4, k),)

    def body(k, carry):
        now, flux_before, bed_before = carry
        after = fetch(jnp.minimum(k + 1, count - 1)) if count > 1 else now
        cell, bed = now[:8], now[8]
        up = tuple(upper(a, b) for a, b in zip(cell, after[:8]))
        y_flux = doubled_flux(swapped(cell), swapped(up))
        y_rolled = tuple(row_roll(f, 1) for f in y_flux)
        dy = tuple(f - lower(b, r) for f, b, r in zip(y_flux, flux_before, y_rolled))
        west = tuple(lane_roll(a, 1) for a in cell)
        x_flux = doubled_flux(west, cell)
        dx = tuple(lane_roll(f, -1) - f for f in x_flux)
        bed_rolled = row_roll(bed, 1)
        bed_y = upper(bed, after[8]) - lower(bed_before, bed_rolled)
        bed_x = lane_roll(bed, -1) - lane_roll(bed, 1)
        h, qx, qy, m = cell[:4]
        friction = load(5, k)
        step = 0.5 * TIME_STEP
        slope = (step * GRAVITY) * h
        new_h = h - step * (dx[0] + dy[0])
        new_x = qx - step * (dx[1] + dy[2]) - slope * bed_x
        new_y = qy - step * (dx[2] + dy[1]) - slope * bed_y
        new_m = m - step * (dx[3] + dy[3])
        inverse = new_h * inverse_of(new_h * new_h + DRY_EPS)
        speed_x = new_x * inverse
        speed_y = new_y * inverse
        square = speed_x * speed_x + speed_y * speed_y
        speed = root_of(square)
        depth = jnp.maximum(new_h, 0.0) + 0.1
        factor = depth * inverse_of(depth + TIME_STEP * friction * speed)
        conc = new_m * inverse
        net = EROSION * jnp.maximum(CAPACITY * square - conc, 0.0) - SETTLING * conc
        store(0, k, new_h)
        store(1, k, new_x * factor)
        store(2, k, new_y * factor)
        store(3, k, new_m + TIME_STEP * net)
        store(4, k, bed - (TIME_STEP / (1.0 - POROSITY)) * net)
        return after, y_rolled, bed_rolled

    zero = jnp.zeros((SUB, LANES), jnp.float32)
    start = (fetch(0), (zero,) * 4, zero)
    if count == 1:
        body(0, start)
    else:
        each = count // slices
        for part in range(slices):
            start = lax.fori_loop(part * each, (part + 1) * each, body, start, unroll=unroll)
            if pause is not None:
                pause(part)


def chunk(k):
    return pl.ds(pl.multiple_of(k * SUB, SUB), SUB)


def pack_frames(patches, frames, turned, with_friction):
    per_dev, _, extent, _ = patches.shape
    fields = 6 if with_friction else 5
    lanes = lane_index()

    def columns(k, _):
        total = jnp.zeros((SUB, LANES), jnp.float32)
        for p in range(per_dev):
            for f in range(fields):
                value = patches[p, f, chunk(k), :]
                base = p * 32
                if f < 4:
                    spots = ((base + 2 * f, 2, 0), (base + 8 + 2 * f, 2, LANES - 2))
                elif f == 4:
                    spots = ((base + 16, 2, 0), (base + 18, 2, LANES - 2))
                else:
                    spots = ((base + 24, 1, 0), (base + 25, 1, LANES - 1))
                for spot, width, origin in spots:
                    inside = (lanes >= spot) & (lanes < spot + width)
                    total = jnp.where(inside, lane_roll(value, spot - origin), total)
        turned[chunk(k), :] = total
        return 0

    lax.fori_loop(0, extent // SUB, columns, 0, unroll=2)
    turned[...] = turned[...].T
    rows = row_index()
    low, high = slice(0, SUB), slice(extent - SUB, extent)
    for p in range(per_dev):
        base = p * 32
        out = frames.at[pl.ds(p * PATCH_TILES, PATCH_TILES)]
        out[WEST] = turned[base : base + 8]
        out[EAST] = turned[base + 8 : base + 16]
        south = north = jnp.zeros((SUB, LANES), jnp.float32)
        for f in range(4):
            inside = (rows >= 2 * f) & (rows < 2 * f + 2)
            south = jnp.where(inside, row_roll(patches[p, f, low, :], 2 * f), south)
            north = jnp.where(inside, row_roll(patches[p, f, high, :], 2 * f + 2), north)
        out[SOUTH] = south
        out[NORTH] = north
        bed = turned[base + 16 : base + 24]
        bed = jnp.where((rows == 4) | (rows == 5), row_roll(patches[p, 4, low, :], 4), bed)
        bed = jnp.where(rows >= 6, patches[p, 4, high, :], bed)
        out[BED_TILE] = bed
        if with_friction:
            rough = turned[base + 24 : base + 32]
            rough = jnp.where(rows == 2, row_roll(patches[p, 5, low, :], 2), rough)
            rough = jnp.where(rows == 3, row_roll(patches[p, 5, high, :], 4), rough)
            if p % 2 == 0:
                paired = rough
            else:
                paired = jnp.where(rows < 4, paired, row_roll(rough, 4))
            if p % 2 == 1 or p == per_dev - 1:
                frames[per_dev * PATCH_TILES + p // 2] = paired


def kept_slots(migration, owner, per_dev):
    moves = migration.shape[0]
    rank = jnp.int32(0)
    slots = [jnp.int32(0)] * (per_dev - moves)
    for slot in range(per_dev):
        stays = jnp.int32(1)
        for k in range(moves):
            stays = stays * jnp.where(migration[k, owner] == slot, 0, 1)
        for j in range(per_dev - moves):
            slots[j] = jnp.where((stays == 1) & (rank == j), slot, slots[j])
        rank = rank + stays
    return slots + [migration[k, owner] for k in range(moves)]


def begin_kernel(device, migration, fields, mask, started, frames, turned):
    per_dev = fields.shape[0]
    slots = kept_slots(migration, device[0], per_dev)
    for p, slot in enumerate(slots):
        wet = mask[slot].astype(jnp.float32)
        for f in range(6):
            started[p, f] = fields[slot, f] * wet if f < 4 else fields[slot, f]
    pack_frames(started, frames, turned, True)


def begin(device, migration, fields, mask):
    per_dev = fields.shape[0]
    return pl.pallas_call(
        begin_kernel,
        out_shape=(
            jax.ShapeDtypeStruct(fields.shape, jnp.float32),
            jax.ShapeDtypeStruct(
                (per_dev * PATCH_TILES + (per_dev + 1) // 2, SUB, LANES), jnp.float32
            ),
        ),
        in_specs=[SMEM, SMEM, VMEM, VMEM],
        out_specs=(VMEM, VMEM),
        scratch_shapes=[pltpu.VMEM((LANES, LANES), jnp.float32)],
        compiler_params=pltpu.CompilerParams(vmem_limit_bytes=VMEM_LIMIT),
    )(device, migration, fields, mask)


def gather_kernel(
    count, moves, patches, mine, pool, main, strip, edges,
    held, middle, own_sem, held_sem, move_send, move_recv, send_sem, recv_sem,
):
    per_dev, _, extent, _ = patches.shape
    chunks = extent // SUB
    length = count // 8
    me = lax.axis_index("curve")
    core, x, y, z = me % 2, (me // 2) % 2, (me // 4) % 2, me // 8
    other_core = me + 1 - 2 * core
    other_x = me + 2 - 4 * x
    other_y = me + 4 - 8 * y
    across = me + 6 - 4 * x - 8 * y
    column = []
    for there, device in ((z >= 1, me - 8), (z + 1 < length, me + 8)):
        column.append((jnp.where(there, device, other_core), there))
    following = lax.rem(me + 1, count)
    previous = lax.rem(me + count - 1, count)

    local = []
    for p in range(per_dev - moves):
        local.append(pltpu.make_async_copy(patches.at[p], held.at[p], held_sem.at[p]))
        local[p].start()
    tiles = mine.shape[0]
    own_copy = pltpu.make_async_copy(mine, pool.at[pl.ds(me * tiles, tiles)], own_sem)
    own_copy.start()

    barrier = pltpu.get_barrier_semaphore()

    def greet(device):
        pl.semaphore_signal(
            barrier, inc=1, device_id=(device,), device_id_type=pl.DeviceIdType.MESH
        )

    friends = [other_core, other_x, other_y] + ([following, previous] if moves else [])
    for device in friends:
        greet(device)
    for device, there in column:
        pl.when(there)(functools.partial(greet, device))
    near = [there.astype(jnp.int32) for _, there in column]
    pl.semaphore_wait(barrier, len(friends) + near[0] + near[1])

    def copy_of(block, device, slot, own):
        target = pool.at[pl.ds(block * tiles, tiles)]
        return pltpu.make_async_remote_copy(
            src_ref=mine if own else target,
            dst_ref=target,
            send_sem=send_sem.at[slot],
            recv_sem=recv_sem.at[block],
            device_id=(device,),
            device_id_type=pl.DeviceIdType.MESH,
        )

    def both(first, second):
        if first is None:
            return second
        return first if second is None else first & second

    def perform(when, action):
        if when is None:
            action()
        else:
            pl.when(when)(action)

    sends = []
    events = {}

    def send(at, block, device, when=None, own=False):
        slot = len(sends)
        sends.append((block, device, slot, own, when))

        def action():
            perform(when, lambda: copy_of(block, device, slot, own).start())

        events.setdefault(at, []).append(action)

    def arrive(at, block, when=None):
        def action():
            perform(when, lambda: copy_of(block, other_core, 0, False).wait_recv())

        events.setdefault(at, []).append(action)

    for device, there in column[::-1] + [(other_x, None), (other_y, None), (other_core, None)]:
        send(-1, me, device, there, True)

    def beside(at, level, when):
        x_block = level * 8 + other_x % 8
        y_block = level * 8 + other_y % 8
        for block, turn, device in (
            (x_block, level % 2 == 0, other_y), (y_block, level % 2 == 1, other_x)
        ):
            arrive(at, block, when)
            send(at, block, device, both(turn, when))
            send(at, block, other_core, when)

    for distance in range(length):
        places = [(z, None)]
        if distance:
            places = [(z - distance, z >= distance), (z + distance, z + distance < length)]
        for sign, (level, there) in zip((-1, 1), places):
            if distance:
                block = level * 8 + me % 8
                at = 6 * distance - 1
                arrive(at, block, there)
                onward, open_way = column[1 if sign < 0 else 0]
                if distance < length - 1:
                    send(at, block, onward, there & open_way)
                for device in (other_x, other_y, other_core):
                    send(at, block, device, there)
            beside(6 * distance + 6, level, there)
            block = level * 8 + across % 8
            arrive(6 * distance + 12, block, there)
            send(6 * distance + 12, block, other_core, there)

    def occur(at):
        for action in events.get(at, ()):
            action()

    occur(-1)
    moving = []
    for k in range(moves):
        moving.append(
            pltpu.make_async_remote_copy(
                src_ref=patches.at[per_dev - moves + k],
                dst_ref=held.at[per_dev - moves + k],
                send_sem=move_send.at[k],
                recv_sem=move_recv.at[k],
                device_id=(following,),
                device_id_type=pl.DeviceIdType.MESH,
            )
        )
        moving[k].start()

    slices = 4
    for copy in local:
        copy.wait()

    def main_patch(p, _):
        for k in range(moves):
            pl.when(p == per_dev - moves + k)(moving[k].wait_recv)
        start, end = held.at[p], main.at[p]
        for step, (source, target) in enumerate(((start, middle), (middle, end))):

            def load(f, k):
                return (start if f == 5 else source)[f, chunk(k), :]

            def store(f, k, value):
                target[f, chunk(k), :] = value

            def pause(part):
                for q in range(per_dev):
                    pl.when(p == q)(lambda: occur(q * 2 * slices + step * slices + part))

            advance_rows(load, store, chunks, 4, slices, pause)
        end[5] = start[5]
        return 0

    lax.fori_loop(0, per_dev, main_patch, 0)

    def fill_strip(k, _):
        for f in range(6):
            strip[f, chunk(k), :] = lay_strip([held[p, f, chunk(k), :] for p in range(per_dev)])
        return 0

    lax.fori_loop(0, chunks, fill_strip, 0, unroll=2)
    for p in range(per_dev):
        for f in range(6):
            edges[p, 0, f] = held[p, f, 0:SUB, :]
            edges[p, 1, f] = held[p, f, extent - SUB : extent, :]

    for at in sorted(events):
        if at >= 2 * slices * per_dev:
            occur(at)
    for square in range(4):
        for level in range(length):
            copy_of(level * 8 + 2 * square + other_core % 2, other_core, 0, False).wait_recv()
    own_copy.wait()
    for copy in moving:
        copy.wait_send()
    for block, device, slot, own, when in sends:
        perform(when, copy_of(block, device, slot, own).wait_send)


def lay_strip(values):
    lanes = lane_index()
    total = jnp.zeros((SUB, LANES), jnp.float32)
    for p, value in enumerate(values):
        for side, shift in ((WEST, 2), (EAST, 6)):
            group = 2 * p + side
            total = jnp.where(lanes // SUB == group, lane_roll(value, group * SUB + shift), total)
    return total


def gather_frames(patches, frames, count, moves, collective_id):
    per_dev, _, extent, _ = patches.shape

    def shape(*sizes):
        return jax.ShapeDtypeStruct(sizes, jnp.float32)

    return pl.pallas_call(
        functools.partial(gather_kernel, count, moves),
        out_shape=(
            shape(count * frames.shape[0], *frames.shape[1:]),
            shape(*patches.shape),
            shape(6, extent, LANES),
            shape(per_dev, 2, 6, SUB, LANES),
        ),
        in_specs=[ANY, ANY],
        out_specs=(ANY, VMEM, VMEM, VMEM),
        scratch_shapes=[
            pltpu.VMEM(patches.shape, jnp.float32),
            pltpu.VMEM((6, extent, LANES), jnp.float32),
            pltpu.SemaphoreType.DMA,
            pltpu.SemaphoreType.DMA((per_dev,)),
            pltpu.SemaphoreType.DMA((max(moves, 1),)),
            pltpu.SemaphoreType.DMA((max(moves, 1),)),
            pltpu.SemaphoreType.DMA((5 * count,)),
            pltpu.SemaphoreType.DMA((count,)),
        ],
        compiler_params=pltpu.CompilerParams(
            collective_id=collective_id, has_side_effects=True, vmem_limit_bytes=VMEM_LIMIT
        ),
    )(patches, frames)


def step_kernel(count, second, device, neighbors, migration, main, own_strip, edges, pool, *refs):
    if second:
        rough_strip, rough_rows, ended, strip_a, strip_b, rows_a, rows_b, turned, halo = refs
    else:
        (ended, frames, rough_strip, rough_rows) = refs[:4]
        (strip_a, strip_b, rows_a, rows_b, turned, halo) = refs[4:]
    held_fields = 5 if second else 6
    per_dev, _, extent, _ = main.shape
    chunks = extent // SUB
    moves = migration.shape[0]
    owner = device[0]
    lanes, rows = lane_index(), row_index()

    def ring(value):
        return jnp.where(value < 0, value + count, jnp.where(value >= count, value - count, value))

    slots = kept_slots(migration, owner, per_dev)
    before = ring(owner - 1)
    held_patches = [owner * per_dev + slot for slot in slots[: per_dev - moves]]
    held_patches += [before * per_dev + migration[k, before] for k in range(moves)]

    tiles = pool.shape[0] // count

    def spot_of(patch):
        home = patch // per_dev
        slot = patch - home * per_dev
        block, place = home, slot
        for k in range(moves):
            place = place - jnp.where(migration[k, home] < slot, 1, 0)
        for k in range(moves):
            here = migration[k, home] == slot
            place = jnp.where(here, per_dev - moves + k, place)
            if second:
                block = jnp.where(here, ring(home + 1), block)
        return block, place

    def tile_of(spot, tile):
        return pool[spot[0] * tiles + spot[1] * PATCH_TILES + tile]

    def friction_of(spot):
        tile = pool[spot[0] * tiles + per_dev * PATCH_TILES + spot[1] // 2]
        return jnp.where(everywhere(spot[1] % 2 == 1), row_roll(tile, 4), tile)

    opposite = {WEST: EAST, EAST: WEST, SOUTH: NORTH, NORTH: SOUTH}

    def repaired(tile, side, missing):
        if side in (WEST, SOUTH):
            return jnp.where(everywhere(missing) & (rows % 2 == 1), row_roll(tile, 1), tile)
        return jnp.where(everywhere(missing) & (rows % 2 == 0), row_roll(tile, -1), tile)

    def bed_lines(source, side, missing):
        bed = tile_of(source, BED_TILE)
        bed = jnp.where(
            everywhere(missing), row_roll(bed, -2 * side), row_roll(bed, -2 * opposite[side])
        )
        return repaired(bed, side, missing)

    def by_field(patch, side, spot, near):
        beyond = neighbors[side, patch]
        missing = beyond < 0
        source = spot_of(jnp.where(missing, patch, beyond))
        edge = jnp.where(missing, side, opposite[side])
        flow = repaired(tile_of(source, edge), side, missing)
        tiles = [row_roll(flow, spot - 2 * f) for f in range(4)]
        tiles.append(row_roll(bed_lines(source, side, missing), spot))
        if not second:
            rough = friction_of(source)
            tiles.append(
                jnp.where(
                    everywhere(missing),
                    row_roll(rough, near - side),
                    row_roll(rough, near - opposite[side]),
                )
            )
        return tiles

    for p in range(per_dev):
        patch = held_patches[p]
        for side, spot, near in ((WEST, 0, 1), (EAST, 6, 6)):
            group = 2 * p + side
            for f, tile in enumerate(by_field(patch, side, spot, near)):
                turned[f, group * SUB : (group + 1) * SUB] = tile
        for end, side, spot, near in ((0, SOUTH, 6, 7), (1, NORTH, 0, 0)):
            for f, tile in enumerate(by_field(patch, side, spot, near)):
                halo[p, end, f] = tile

    for f in range(held_fields):
        turned[f] = turned[f].T

    group_lane = lanes % SUB
    odd_group = (lanes // SUB) % 2
    from_halo = ((odd_group == 0) & (group_lane < 2)) | ((odd_group == 1) & (group_lane >= 6))

    def fill_strip(k, _):
        for f in range(held_fields):
            strip_a[f, chunk(k + 1), :] = jnp.where(
                from_halo, turned[f, chunk(k), :], own_strip[f, chunk(k), :]
            )
        return 0

    lax.fori_loop(0, chunks, fill_strip, 0, unroll=2)

    for end, side, row, line in ((0, SOUTH, 7, 1), (1, NORTH, 0, 0)):
        place = slice(0, SUB) if end == 0 else slice((chunks + 1) * SUB, (chunks + 2) * SUB)
        corner = [
            lay_strip([halo[p, end, f] for p in range(per_dev)]) for f in range(held_fields)
        ]
        for p in range(per_dev):
            patch = held_patches[p]
            beyond = neighbors[side, patch]
            missing = beyond < 0
            base = jnp.where(missing, patch, beyond)
            edge = jnp.where(missing, side, opposite[side])
            for across, spot, inner, outer in ((WEST, 1, 0, LANES - 1), (EAST, 6, LANES - 1, 0)):
                aside = neighbors[across, base]
                alone = everywhere(aside < 0)
                source = spot_of(jnp.where(aside < 0, base, aside))
                lane = (2 * p + across) * SUB + spot
                flow = repaired(tile_of(source, edge), side, missing)
                bed = bed_lines(source, side, missing)
                flow = jnp.where(alone, lane_roll(flow, lane - inner), lane_roll(flow, lane - outer))
                bed = jnp.where(alone, lane_roll(bed, lane - inner), lane_roll(bed, lane - outer))
                here = (lanes == lane) & (rows == row)
                for f in range(4):
                    corner[f] = jnp.where(here, row_roll(flow, row - 2 * f - line), corner[f])
                corner[4] = jnp.where(here, row_roll(bed, row - line), corner[4])
        for f in range(held_fields):
            strip_a[f, place, :] = corner[f]

    for p in range(per_dev):
        for f in range(held_fields):
            rows_a[2 * p, f] = jnp.where(
                rows < 2, row_roll(halo[p, 0, f], 2), row_roll(edges[p, 0, f], 2)
            )
            rows_a[2 * p + 1, f] = jnp.where(
                rows >= 6, row_roll(halo[p, 1, f], 6), row_roll(edges[p, 1, f], -2)
            )

    if not second:
        rough_strip[...] = strip_a[5]
        for i in range(2 * per_dev):
            rough_rows[i] = rows_a[i, 5]

    def run(source, target):
        def load(f, k):
            return rough_strip[chunk(k), :] if f == 5 else source[f, chunk(k), :]

        def store(f, k, value):
            target[f, chunk(k), :] = value

        advance_rows(load, store, chunks + 2, 2)

    run(strip_a, strip_b)
    run(strip_b, strip_a)

    def row_strip(i, _):
        def step(source, target):
            def load(f, k):
                return rough_rows[i] if f == 5 else source[i, f]

            def store(f, k, value):
                target[i, f] = value

            advance_rows(load, store, 1, 1)

        step(rows_a, rows_b)
        step(rows_b, rows_a)
        return 0

    lax.fori_loop(0, 2 * per_dev, row_strip, 0, unroll=2)

    ends = slots if second else list(range(per_dev))

    def merge(k, _):
        for f in range(5):
            strip = strip_a[f, chunk(k + 1), :]
            for p in range(per_dev):
                value = main[p, f, chunk(k), :]
                value = jnp.where(
                    (rows < 2) & everywhere(k == 0), row_roll(rows_a[2 * p, f], -2), value
                )
                value = jnp.where(
                    (rows >= 6) & everywhere(k == chunks - 1),
                    row_roll(rows_a[2 * p + 1, f], 2),
                    value,
                )
                west = lane_roll(strip, -(2 * p * SUB + 2))
                east = lane_roll(strip, -6 - (2 * p + 1) * SUB)
                value = jnp.where(lanes < 2, west, value)
                ended[ends[p], f, chunk(k), :] = jnp.where(lanes >= LANES - 2, east, value)
        for p in range(per_dev):
            ended[ends[p], 5, chunk(k), :] = main[p, 5, chunk(k), :]
        return 0

    lax.fori_loop(0, chunks, merge, 0)
    if not second:
        pack_frames(ended, frames, turned.at[0], False)


def finish_round(device, neighbors, migration, pieces, count, rough):
    pool, main, strip, edges = pieces
    second = rough is not None
    per_dev, _, extent, _ = main.shape

    def shape(*sizes):
        return jax.ShapeDtypeStruct(sizes, jnp.float32)

    rough_shapes = (shape(extent + 2 * SUB, LANES), shape(2 * per_dev, SUB, LANES))
    out_shape = (shape(*main.shape),)
    if not second:
        out_shape += (shape(per_dev * PATCH_TILES, SUB, LANES),) + rough_shapes
    operands = (device, neighbors, migration, main, strip, edges, pool)
    if second:
        operands += rough
    return pl.pallas_call(
        functools.partial(step_kernel, count, second),
        out_shape=out_shape,
        in_specs=[SMEM] * 3 + [VMEM] * (len(operands) - 3),
        out_specs=(VMEM,) * len(out_shape),
        scratch_shapes=[
            pltpu.VMEM((6, extent + 2 * SUB, LANES), jnp.float32),
            pltpu.VMEM((6, extent + 2 * SUB, LANES), jnp.float32),
            pltpu.VMEM((2 * per_dev, 6, SUB, LANES), jnp.float32),
            pltpu.VMEM((2 * per_dev, 6, SUB, LANES), jnp.float32),
            pltpu.VMEM((6, LANES, LANES), jnp.float32),
            pltpu.VMEM((per_dev, 2, 6, SUB, LANES), jnp.float32),
        ],
        compiler_params=pltpu.CompilerParams(vmem_limit_bytes=VMEM_LIMIT),
    )(*operands)


def shards(fields, wet_mask, neighbors, migration):
    count = lax.axis_size("curve")
    moves = migration.shape[1]
    device = lax.axis_index("curve").astype(jnp.int32).reshape(1)
    neighbors, migration = neighbors.T, migration.T
    started, frames = begin(device, migration, fields, wet_mask)
    pieces = gather_frames(started, frames, count, moves, 0)
    halfway, frames, *rough = finish_round(device, neighbors, migration, pieces, count, None)
    pieces = gather_frames(halfway, frames, count, 0, 1)
    (ended,) = finish_round(device, neighbors, migration, pieces, count, tuple(rough))
    return ended


def solution(mesh):
    placed = (P("curve", None, None, None), P("curve", None, None), P(), P())
    return jax.shard_map(
        shards, mesh=mesh, in_specs=placed, out_specs=P("curve", None, None, None), check_vma=False
    )
```
